32 devices in a mesh: wide: 8 (over y, x, core), narrow: 4 (over z).
Axes of the slice: x: 2, y: 2, z: 4, core: 2. Of those that a mesh axis runs over, the one named last changes fastest.
Arguments:
- tokens: bfloat16 [8, 4, 128, 1152], P(None, 'narrow', 'wide'), may hold values from -6 to 6
- cotangent: bfloat16 [8, 4, 128, 1152], P(None, 'narrow', 'wide'), may hold values from -6 to 6
- seq_lengths: int32 [8, 2], P('wide'), may hold values from 0 to 512, as said below
- query_weight: bfloat16 [1152, 1024], P('wide', 'narrow'), may hold values from -0.1875 to 0.1875
- key_weight: bfloat16 [1152, 256], P('wide'), may hold values from -0.1875 to 0.1875
- value_weight: bfloat16 [1152, 256], P('wide'), may hold values from -0.1875 to 0.1875
- outproj_weight: bfloat16 [1152, 1024], P('wide', 'narrow'), may hold values from -0.1875 to 0.1875
- gate_weight: bfloat16 [1152, 6912], P('wide', 'narrow'), may hold values from -0.1875 to 0.1875
- up_weight: bfloat16 [1152, 6912], P('wide', 'narrow'), may hold values from -0.1875 to 0.1875
- down_weight: bfloat16 [1152, 6912], P('wide', 'narrow'), may hold values from -0.078125 to 0.078125
- attn_gain: bfloat16 [1152], P('wide'), may hold values from -0.5 to 0.5
- attnout_gain: bfloat16 [1152], P('wide'), may hold values from -0.5 to 0.5
- ffn_gain: bfloat16 [1152], P('wide'), may hold values from -0.5 to 0.5
- ffnout_gain: bfloat16 [1152], P('wide'), may hold values from -0.5 to 0.5
- query_gain: bfloat16 [256], P('wide'), may hold values from -0.5 to 0.5
- key_gain: bfloat16 [256], P('wide'), may hold values from -0.5 to 0.5
Outputs:
- layer_out: bfloat16 [8, 4, 128, 1152], P(None, 'narrow', 'wide')
- input_grad: bfloat16 [8, 4, 128, 1152], P(None, 'narrow', 'wide')
- query_grad: float32 [1152, 1024], P('wide', 'narrow')
- key_grad: float32 [1152, 256], P('wide')
- value_grad: float32 [1152, 256], P('wide')
- outproj_grad: float32 [1152, 1024], P('wide', 'narrow')
- gate_grad: float32 [1152, 6912], P('wide', 'narrow')
- up_grad: float32 [1152, 6912], P('wide', 'narrow')
- down_grad: float32 [1152, 6912], P('wide', 'narrow')
- attngain_grad: float32 [1152], P('wide')
- attnoutgain_grad: float32 [1152], P('wide')
- ffngain_grad: float32 [1152], P('wide')
- ffnoutgain_grad: float32 [1152], P('wide')
- querygain_grad: float32 [256], P('wide')
- keygain_grad: float32 [256], P('wide')
The draws below stay inside these ranges and needn't reach their ends.
Inputs may be any that keep to these rules, and one draw needn't show every extreme that they name: `seq_lengths`: row b holds the lengths of the two sequences that stand in order at the start of bucket b, the rest of the bucket being padding; the longer exceeds 3 * 128, the two sum to at most 512, and in every draw some bucket holds one sequence of 512 tokens.
All inputs are finite; a program needn't handle non-finite values.
Results may differ from the reference program's by a relative error of at most 0.025.
Values may be sent and summed in bfloat16 or wider, within the bound.
No kernel may reach another device: no remote copies, remote signals or barrier semaphores. Data moves between devices by JAX's collectives and lax.ppermute only.
A program may use at most 192 MiB of HBM per device.

```python
import math
import jax
import jax.numpy as jnp
from jax import lax

D = 1152
HEADS = 4
HEAD = 256
FF = 6912
TOK_DEV = 128
BUCKETS = 8
QUARTERS = 4
BLEN = 512


def draw_seq_lengths(key, part):
    keys = jax.random.split(key, 4)
    longer = jax.random.randint(keys[0], (BUCKETS,), 3 * BLEN // 4 + 1, BLEN + 1)
    spare = BLEN - longer
    shorter = jax.random.randint(keys[1], (BUCKETS,), 0, BLEN + 1) % (spare + 1)
    chosen = jax.random.randint(keys[2], (), 0, BUCKETS)
    marks = jnp.arange(BUCKETS) == chosen
    longer = jnp.where(marks, BLEN, longer)
    shorter = jnp.where(marks, 0, shorter)
    flips = jax.random.randint(keys[3], (BUCKETS,), 0, 2)
    first = jnp.where(flips == 1, shorter, longer)
    second = jnp.where(flips == 1, longer, shorter)
    return jnp.stack([first, second], axis=1).astype(jnp.int32)


def block_scale(stream_key, extent, shards, smallest, high):
    level, own = 1.0, jax.random.fold_in(stream_key, 6)
    for axis_at, parts in shards:
        steps = jnp.exp(jax.random.uniform(jax.random.fold_in(own, axis_at), (parts,), jnp.float32, smallest / len(shards), high / len(shards)))
        level = level * jnp.repeat(steps, extent[axis_at] // parts).reshape([-1 if axis == axis_at else 1 for axis in range(len(extent))])
    return level


def centred(rng, dims, spread, most, shards=(), held_as=jnp.bfloat16):
    entries = spread * jax.random.normal(rng, dims, jnp.float32)
    if shards:
        entries = entries * block_scale(rng, dims, shards, -0.22, 0.18)
    return jnp.clip(entries, -most, most).astype(held_as)


def setup_inputs(seed: int = 0) -> dict:
    seeds = jax.random.split(jax.random.key(seed), 17)
    tokens = centred(seeds[0], (BUCKETS, QUARTERS, TOK_DEV, D), 1.0, 6.0, ((1, 4), (2, 8)))
    cotangent = centred(seeds[1], (BUCKETS, QUARTERS, TOK_DEV, D), 1.0, 6.0, ((1, 4), (2, 8)))
    seq_lengths = draw_seq_lengths(jax.random.fold_in(seeds[16], 71), 0)
    query_weight = centred(seeds[3], (D, HEADS * HEAD), D ** -0.5, 0.1875, ((0, 8), (1, 4)))
    key_weight = centred(seeds[4], (D, HEAD), D ** -0.5, 0.1875, ((0, 8),))
    value_weight = centred(seeds[5], (D, HEAD), D ** -0.5, 0.1875, ((0, 8),))
    outproj_weight = centred(seeds[6], (D, HEADS * HEAD), (HEADS * HEAD) ** -0.5, 0.1875, ((0, 8), (1, 4)))
    gate_weight = centred(seeds[7], (D, FF), D ** -0.5, 0.1875, ((0, 8), (1, 4)))
    up_weight = centred(seeds[8], (D, FF), D ** -0.5, 0.1875, ((0, 8), (1, 4)))
    down_weight = centred(seeds[9], (D, FF), FF ** -0.5, 0.078125, ((0, 8), (1, 4)))
    attn_gain = jnp.clip(jax.random.uniform(seeds[10], (D,), jnp.float32, -0.5, 0.5) * block_scale(seeds[10], (D,), ((0, 8),), -0.4, 0.0), -0.5, 0.5).astype(jnp.bfloat16)
    attnout_gain = jnp.clip(jax.random.uniform(seeds[11], (D,), jnp.float32, -0.5, 0.5) * block_scale(seeds[11], (D,), ((0, 8),), -0.4, 0.0), -0.5, 0.5).astype(jnp.bfloat16)
    ffn_gain = jnp.clip(jax.random.uniform(seeds[12], (D,), jnp.float32, -0.5, 0.5) * block_scale(seeds[12], (D,), ((0, 8),), -0.4, 0.0), -0.5, 0.5).astype(jnp.bfloat16)
    ffnout_gain = jnp.clip(jax.random.uniform(seeds[13], (D,), jnp.float32, -0.5, 0.5) * block_scale(seeds[13], (D,), ((0, 8),), -0.4, 0.0), -0.5, 0.5).astype(jnp.bfloat16)
    query_gain = jnp.clip(jax.random.uniform(seeds[14], (HEAD,), jnp.float32, -0.5, 0.5) * block_scale(seeds[14], (HEAD,), ((0, 8),), -0.4, 0.0), -0.5, 0.5).astype(jnp.bfloat16)
    key_gain = jnp.clip(jax.random.uniform(seeds[15], (HEAD,), jnp.float32, -0.5, 0.5) * block_scale(seeds[15], (HEAD,), ((0, 8),), -0.4, 0.0), -0.5, 0.5).astype(jnp.bfloat16)
    return {"tokens": tokens, "cotangent": cotangent, "seq_lengths": seq_lengths, "query_weight": query_weight, "key_weight": key_weight, "value_weight": value_weight, "outproj_weight": outproj_weight, "gate_weight": gate_weight, "up_weight": up_weight, "down_weight": down_weight, "attn_gain": attn_gain, "attnout_gain": attnout_gain, "ffn_gain": ffn_gain, "ffnout_gain": ffnout_gain, "query_gain": query_gain, "key_gain": key_gain}


EPS = 1e-06
SCALE = 0.0625
LOGBASE = math.log(1000000.0)
HIGH = lax.Precision.HIGHEST

@jax.custom_vjp
def low(v):
    return lax.optimization_barrier(v.astype(jnp.bfloat16)).astype(jnp.float32)

@jax.custom_vjp
def low_back(v):
    return v

def low_keep(v):
    return (low(v), None)

def low_pass(kept, grad):
    return (grad,)

def back_keep(v):
    return (v, None)

def back_low(kept, grad):
    return (low(grad),)
low.defvjp(low_keep, low_pass)
low_back.defvjp(back_keep, back_low)

def norm_gain(value, gain):
    return value * lax.rsqrt(lax.optimization_barrier(jnp.mean(value * value, axis=-1, keepdims=True)) + EPS) * (1.0 + gain)

def gelu_tanh(value):
    return 0.5 * value * (1.0 + jnp.tanh(0.7978845608028654 * (value + 0.044715 * value * value * value)))

def rope_tables(place, width):
    half = width // 2
    expo = jnp.arange(half, dtype=jnp.float32) * (-2.0 / width)
    freqs = jnp.exp(expo * LOGBASE)
    angle = place.astype(jnp.float32)[:, None] * freqs[None, :]
    return (jnp.cos(angle), jnp.sin(angle))

def rotate(value, cosine, sine):
    half = value.shape[-1] // 2
    first = value[..., :half]
    second = value[..., half:]
    return jnp.concatenate([first * cosine - second * sine, second * cosine + first * sine], axis=-1)

def bucket_layout(lengths, rows):
    position = jnp.arange(rows, dtype=jnp.int32)
    first = lengths[0].astype(jnp.int32)
    ends = (lengths[0] + lengths[1]).astype(jnp.int32)
    segment = jnp.where(position < first, 0, jnp.where(position < ends, 1, 2)).astype(jnp.int32)
    begin = jnp.where(segment == 0, 0, jnp.where(segment == 1, first, ends)).astype(jnp.int32)
    return (segment, position - begin)

def layer(x_rows, params, segment, place):
    query_w, key_w, value_w, outproj_w, gate_w, up_w, down_w, attn_g, attnout_g, ffn_g, ffnout_g, query_g, key_g = params
    rows = x_rows.shape[0]
    block = min(512, rows)
    xn1 = low(norm_gain(x_rows, attn_g))
    q_raw = low_back(jnp.dot(xn1, query_w, precision=HIGH)).reshape(rows, HEADS, HEAD)
    k_raw = low_back(jnp.dot(xn1, key_w, precision=HIGH))
    values = low(low_back(jnp.dot(xn1, value_w, precision=HIGH)))
    cosine, sine = rope_tables(place, HEAD)
    queries = low(low_back(rotate(norm_gain(q_raw, query_g), cosine[:, None, :], sine[:, None, :])))
    keys = low(low_back(rotate(norm_gain(k_raw, key_g), cosine, sine)))
    key_pos = jnp.arange(rows, dtype=jnp.int32)

    def attend(index):
        start = (index * block).astype(jnp.int32)
        q_block = lax.dynamic_slice_in_dim(queries, start, block, 0)
        seg_block = lax.dynamic_slice_in_dim(segment, start, block, 0)
        row_pos = start + jnp.arange(block, dtype=jnp.int32)
        allowed = (seg_block[:, None] == segment[None, :]) & (key_pos[None, :] <= row_pos[:, None])
        scores = low_back(jnp.einsum('qhd,kd->hqk', q_block, keys, precision=HIGH) * SCALE)
        scores = jnp.where(allowed[None], scores, -1e+30)
        top = lax.optimization_barrier(jnp.max(scores, axis=-1, keepdims=True))
        raised = jnp.exp(scores - top)
        probs = low(raised / lax.optimization_barrier(jnp.sum(raised, axis=-1, keepdims=True)))
        return jnp.einsum('hqk,kd->qhd', probs, values, precision=HIGH)
    blocks = lax.map(jax.checkpoint(attend), jnp.arange(rows // block, dtype=jnp.int32))
    attended = low(low_back(blocks.reshape(rows, HEADS * HEAD)))
    mixed = low_back(jnp.dot(attended, outproj_w.T, precision=HIGH))
    resid = x_rows + norm_gain(mixed, attnout_g)
    xn2 = low(norm_gain(resid, ffn_g))
    gate = low_back(jnp.dot(xn2, gate_w, precision=HIGH))
    up = low_back(jnp.dot(xn2, up_w, precision=HIGH))
    act = low(gelu_tanh(gate) * up)
    ffn_out = low_back(jnp.dot(act, down_w.T, precision=HIGH))
    return resid + norm_gain(ffn_out, ffnout_g)

def reference(tokens, cotangent, seq_lengths, query_weight, key_weight, value_weight, outproj_weight, gate_weight, up_weight, down_weight, attn_gain, attnout_gain, ffn_gain, ffnout_gain, query_gain, key_gain):
    params = tuple((w.astype(jnp.float32) for w in (query_weight, key_weight, value_weight, outproj_weight, gate_weight, up_weight, down_weight, attn_gain, attnout_gain, ffn_gain, ffnout_gain, query_gain, key_gain)))
    inputs = tokens.astype(jnp.float32).reshape(BUCKETS, BLEN, D)
    grads_in = cotangent.astype(jnp.float32).reshape(BUCKETS, BLEN, D)

    def one_bucket(totals, item):
        x_rows, dy_rows, lengths = item
        segment, place = bucket_layout(lengths, BLEN)
        valid = (segment < 2).astype(jnp.float32)
        out_rows, pullback = jax.vjp(lambda rows_in, weights_in: layer(rows_in, weights_in, segment, place), x_rows, params)
        dx_rows, dparams = pullback(dy_rows * valid[:, None])
        totals = tuple((t + g for t, g in zip(totals, dparams)))
        return (totals, (out_rows.astype(jnp.bfloat16), dx_rows.astype(jnp.bfloat16)))
    zeros = tuple((jnp.zeros(p.shape, jnp.float32) for p in params))
    totals, (outs, dxs) = lax.scan(one_bucket, zeros, (inputs, grads_in, seq_lengths))
    shape = (BUCKETS, QUARTERS, TOK_DEV, D)
    return (outs.reshape(shape), dxs.reshape(shape), totals[0], totals[1], totals[2], totals[3], totals[4], totals[5], totals[6], totals[7], totals[8], totals[9], totals[10], totals[11], totals[12])
```

```python
import functools
import math

import jax
import jax.numpy as jnp
from jax import lax
from jax.experimental import pallas as pl
from jax.experimental.pallas import tpu as pltpu
from jax.sharding import PartitionSpec as P

EPS = 1e-06
SCALE = 0.0625
LOGBASE = math.log(1000000.0)
GELU_C = 0.7978845608028654
GELU_A = 0.044715
F32, BF16 = jnp.float32, jnp.bfloat16
VMEM_LIMIT = 60 * 1024 * 1024


def call(kernel, outs, scratch=(), anys=(), smem=(), count=0, flops=0, moved=0):
    def place(index):
        if index in anys:
            return pl.BlockSpec(memory_space=pl.ANY)
        if index in smem:
            return pl.BlockSpec(memory_space=pltpu.SMEM)
        return pl.BlockSpec(memory_space=pltpu.VMEM)

    return pl.pallas_call(
        kernel,
        out_shape=[jax.ShapeDtypeStruct(s, d) for s, d in outs],
        in_specs=[place(i) for i in range(count)],
        out_specs=[pl.BlockSpec(memory_space=pltpu.VMEM)] * len(outs),
        scratch_shapes=list(scratch),
        compiler_params=pltpu.CompilerParams(vmem_limit_bytes=VMEM_LIMIT),
        cost_estimate=pl.CostEstimate(flops=flops, bytes_accessed=moved, transcendentals=0),
    )


def mm(a, b):
    return lax.dot_general(a, b, (((1,), (0,)), ((), ())), preferred_element_type=F32)


def mm_nt(a, b):
    return lax.dot_general(a, b, (((1,), (1,)), ((), ())), preferred_element_type=F32)


def mm_tn(a, b):
    return lax.dot_general(a, b, (((0,), (0,)), ((), ())), preferred_element_type=F32)


def root(v):
    return lax.rsqrt(jnp.mean(v * v, axis=-1, keepdims=True) + EPS)


def norm(v, gain):
    return v * root(v) * (1.0 + gain)


def norm_back(v, grad, gain):
    r = root(v)
    e = grad * (1.0 + gain)
    return r * e - v * (r * r * r * jnp.mean(e * v, axis=-1, keepdims=True))


def norm_term(v, grad):
    return jnp.sum(grad * v * root(v), axis=0, keepdims=True)


def rotate(v, cosine, sine):
    half = v.shape[-1] // 2
    a, b = v[:, :half], v[:, half:]
    return jnp.concatenate([a * cosine - b * sine, b * cosine + a * sine], axis=-1)


def rotate_back(v, cosine, sine):
    half = v.shape[-1] // 2
    a, b = v[:, :half], v[:, half:]
    return jnp.concatenate([a * cosine + b * sine, b * cosine - a * sine], axis=-1)


def tiles(extent, size):
    return [(i, min(size, extent - i)) for i in range(0, extent, size)]


def packing(q_ref, k_ref, v_ref, o_ref, g0_ref, g1_ref, g2_ref, g3_ref, g4_ref, g5_ref, out_ref):
    rows, head = q_ref.shape
    for i, ref in enumerate((q_ref, k_ref, v_ref, o_ref)):
        out_ref[:, i * head : (i + 1) * head] = ref[...]
    lane = lax.broadcasted_iota(jnp.int32, (rows, 128), 1)
    columns = jnp.zeros((rows, 128), F32)
    for i, ref in enumerate((g0_ref, g1_ref, g2_ref, g3_ref, g4_ref, g5_ref)):
        n = ref.shape[0]
        same = lax.broadcasted_iota(jnp.int32, (rows, n), 0) == lax.broadcasted_iota(
            jnp.int32, (rows, n), 1
        )
        column = jnp.sum(jnp.where(same, ref[...].astype(F32)[None, :], 0.0), axis=1, keepdims=True)
        columns = jnp.where(lane == i, column, columns)
    out_ref[:, 4 * head :] = columns.astype(BF16)


def one_hot(order_ref, rows):
    index = lax.broadcasted_iota(jnp.int32, (rows, order_ref.shape[1]), 0)
    return jnp.where(index == order_ref[...], 1.0, 0.0).astype(BF16)


def fetch(pieces, slot, target, sem):
    own, below, above = pieces
    n, count = own.shape[0], len(below) + 1

    def copy(ref, at, i):
        at = pl.multiple_of(at * n, n)
        return pltpu.make_async_copy(ref, target.at[pl.ds(at, n)], sem.at[i])

    def each(act):
        act(copy(own, slot, 0))
        for s in range(1, count):

            @pl.when(slot >= s)
            def _(s=s):
                act(copy(below[s - 1], slot - s, 2 * s - 1))

            @pl.when(slot + s < count)
            def _(s=s):
                act(copy(above[s - 1], slot + s, 2 * s))

    each(lambda c: c.start())
    return lambda: each(lambda c: c.wait())


def attention_forward(
    own_ref, b1_ref, b2_ref, b3_ref, a1_ref, a2_ref, a3_ref,
    order_ref, pick_ref, wm_ref, wo_ref, cos_ref, sin_ref, segc_ref, segr_ref, slot_ref,
    xp_ref, xn1_ref, qraw_ref, kraw_ref, q_ref, k_ref, v_ref, probs_ref, att_ref, part_ref,
    gains_ref, hgain_ref,
    x_ref, w_ref, sem, xsem,
):
    half, head = wm_ref.shape[0], q_ref.shape[1]
    rows, width = x_ref.shape
    arrived = fetch(
        (own_ref, (b1_ref, b2_ref, b3_ref), (a1_ref, a2_ref, a3_ref)), slot_ref[0], x_ref, xsem
    )
    low = pltpu.make_async_copy(wm_ref, w_ref.at[pl.ds(0, half)], sem.at[0])
    high = pltpu.make_async_copy(wo_ref, w_ref.at[pl.ds(half, half)], sem.at[1])
    low.start()
    high.start()
    choose = one_hot(order_ref, width)
    low.wait()
    high.wait()
    columns = w_ref[:, 4 * head :].T
    gains_ref[...] = columns[:8].astype(F32)
    hgain_ref[...] = mm(columns[:8], one_hot(pick_ref, width))
    arrived()
    step = 128
    for r, n in tiles(rows, step):
        x = mm(x_ref[pl.ds(r, n), :], choose)
        xp_ref[pl.ds(r, n), :] = x.astype(BF16)
        xn1_ref[pl.ds(r, n), :] = norm(x, gains_ref[0:1, :]).astype(BF16)
    gq, gk = hgain_ref[4:5, :], hgain_ref[5:6, :]
    raw = mm(xn1_ref[...], w_ref[:, : 3 * head])
    qraw_ref[...] = raw[:, :head]
    kraw_ref[...] = raw[:, head : 2 * head]
    v_ref[...] = raw[:, 2 * head :].astype(BF16)
    cosine, sine = cos_ref[...], sin_ref[...]
    q_ref[...] = rotate(norm(raw[:, :head], gq), cosine, sine).astype(BF16)
    k_ref[...] = rotate(norm(raw[:, head : 2 * head], gk), cosine, sine).astype(BF16)
    for r, n in tiles(rows, step):
        s = mm_nt(q_ref[pl.ds(r, n), :], k_ref[...]) * SCALE
        row = lax.broadcasted_iota(jnp.int32, s.shape, 0) + r
        col = lax.broadcasted_iota(jnp.int32, s.shape, 1)
        keep = (segc_ref[pl.ds(r, n), :] == segr_ref[...]) & (col <= row)
        s = jnp.where(keep, s, -1e30)
        e = jnp.exp(s - jnp.max(s, axis=-1, keepdims=True))
        p = e / jnp.sum(e, axis=-1, keepdims=True)
        probs_ref[pl.ds(r, n), :] = p
        att_ref[pl.ds(r, n), :] = mm(p.astype(BF16), v_ref[...]).astype(BF16)
    part_ref[...] = mm_nt(att_ref[...], w_ref[:, 3 * head : 4 * head]).astype(BF16)


def total(ref):
    out = ref[0].astype(F32)
    for i in range(1, ref.shape[0]):
        out = out + ref[i].astype(F32)
    return out


def middle_forward(z_ref, xp_ref, gains_ref, slot_ref, mixed_ref, h_ref, xn2_ref):
    n = h_ref.shape[0]
    x = xp_ref[pl.ds(pl.multiple_of(slot_ref[0] * n, n), n), :].astype(F32)
    z = total(z_ref)
    h = x + norm(z, gains_ref[1:2, :])
    mixed_ref[...] = z
    h_ref[...] = h
    xn2_ref[...] = norm(h, gains_ref[2:3, :]).astype(BF16)


def ffn_forward(
    own_ref, b1_ref, b2_ref, b3_ref, a1_ref, a2_ref, a3_ref, wm_ref, wo_ref, slot_ref,
    xn2_ref, act_ref, fa_ref, fb_ref, part_ref, w_ref, sem, xsem,
):
    half = wm_ref.shape[1]
    arrived = fetch(
        (own_ref, (b1_ref, b2_ref, b3_ref), (a1_ref, a2_ref, a3_ref)), slot_ref[0], xn2_ref, xsem
    )
    copies = []
    for i in range(3):
        for j, ref in enumerate((wm_ref, wo_ref)):
            c = pltpu.make_async_copy(
                ref.at[i], w_ref.at[i, pl.ds(j * half, half)], sem.at[2 * i + j]
            )
            c.start()
            copies.append(c)
    for c in copies[:4]:
        c.wait()
    arrived()
    x = xn2_ref[...]
    for f, n in tiles(act_ref.shape[1], 256):
        gate = mm(x, w_ref[0, :, pl.ds(f, n)])
        up = mm(x, w_ref[1, :, pl.ds(f, n)])
        square = gate * gate
        t = jnp.tanh(GELU_C * (gate + GELU_A * (gate * square)))
        bell = 0.5 * (1.0 + t)
        g = gate * bell
        slope = bell + 0.5 * gate * (1.0 - t * t) * (GELU_C * (1.0 + 3.0 * GELU_A * square))
        act_ref[:, pl.ds(f, n)] = (g * up).astype(BF16)
        fa_ref[:, pl.ds(f, n)] = (slope * up).astype(BF16)
        fb_ref[:, pl.ds(f, n)] = g.astype(BF16)
    for c in copies[4:]:
        c.wait()
    for d, n in tiles(part_ref.shape[1], 384):
        part_ref[:, pl.ds(d, n)] = mm_nt(act_ref[...], w_ref[2, pl.ds(d, n), :]).astype(BF16)


def middle_turn(
    m_ref, h_ref, dy_ref, order_ref, valid_ref, gains_ref, out_ref, dout_ref, dm_ref, term_ref
):
    choose = one_hot(order_ref, h_ref.shape[1])
    m = total(m_ref)
    gain = gains_ref[3:4, :]
    out = (h_ref[...] + norm(m, gain)).astype(BF16)
    out_ref[...] = mm_nt(out, choose).astype(BF16)
    dy = mm(dy_ref[...], choose) * valid_ref[...]
    dout_ref[...] = dy
    dm_ref[...] = norm_back(m, dy, gain).astype(BF16)
    term_ref[...] = norm_term(m, dy)


def ffn_backward(
    own_ref, b1_ref, b2_ref, b3_ref, a1_ref, a2_ref, a3_ref, fa_ref, fb_ref, wm_ref, wo_ref, slot_ref,
    dm_ref, dg_ref, du_ref, part_ref, w_ref, sem, xsem,
):
    half = wm_ref.shape[1]
    arrived = fetch(
        (own_ref, (b1_ref, b2_ref, b3_ref), (a1_ref, a2_ref, a3_ref)), slot_ref[0], dm_ref, xsem
    )
    copies = []
    for i in (2, 0, 1):
        for j, ref in enumerate((wm_ref, wo_ref)):
            c = pltpu.make_async_copy(
                ref.at[i], w_ref.at[i, pl.ds(j * half, half)], sem.at[2 * i + j]
            )
            c.start()
            copies.append(c)
    for c in copies[:2]:
        c.wait()
    arrived()
    dm = dm_ref[...]
    for f, n in tiles(dg_ref.shape[1], 256):
        d = mm(dm, w_ref[2, :, pl.ds(f, n)])
        dg_ref[:, pl.ds(f, n)] = (d * fa_ref[:, pl.ds(f, n)].astype(F32)).astype(BF16)
        du_ref[:, pl.ds(f, n)] = (d * fb_ref[:, pl.ds(f, n)].astype(F32)).astype(BF16)
    for c in copies[2:]:
        c.wait()
    for d, n in tiles(part_ref.shape[1], 384):
        part_ref[:, pl.ds(d, n)] = (
            mm_nt(dg_ref[...], w_ref[0, pl.ds(d, n), :])
            + mm_nt(du_ref[...], w_ref[1, pl.ds(d, n), :])
        ).astype(BF16)


def weight_grad(left_ref, right_ref, own_ref, other_ref, turned_ref):
    turned_ref[...] = left_ref[...].T
    half = own_ref.shape[0]
    for r, n in tiles(half, 192):
        for at, out in ((r, own_ref), (half + r, other_ref)):
            out[pl.ds(r, n), :] = mm(turned_ref[pl.ds(at, n), :], right_ref[...]).astype(BF16)


def ffn_weight_grads(
    dm_ref, xn2_ref, act_ref, dg_ref, du_ref, own_ref, other_ref, turned_ref, sem
):
    half = own_ref.shape[1]
    for i, (left, right) in enumerate(((xn2_ref, dg_ref), (xn2_ref, du_ref), (dm_ref, act_ref))):
        if i != 1:
            turned_ref[...] = left[...].T
        for r, n in tiles(half, 192):
            for at, out in ((r, own_ref), (half + r, other_ref)):
                out[i, pl.ds(r, n), :] = mm(turned_ref[pl.ds(at, n), :], right[...]).astype(BF16)


def middle_backward(
    g_ref, dout_ref, h_ref, mixed_ref, gains_ref, dh_ref, dz_ref, ffn_term_ref, att_term_ref
):
    dxn2 = total(g_ref)
    h = h_ref[...]
    dh = dout_ref[...] + norm_back(h, dxn2, gains_ref[2:3, :])
    mixed = mixed_ref[...]
    dh_ref[...] = dh
    dz_ref[...] = norm_back(mixed, dh, gains_ref[1:2, :]).astype(BF16)
    ffn_term_ref[...] = norm_term(h, dxn2)
    att_term_ref[...] = norm_term(mixed, dh)


def attention_backward(
    own_ref, b1_ref, b2_ref, b3_ref, a1_ref, a2_ref, a3_ref, slot_ref, wm_ref, wo_ref, qraw_ref, q_ref, k_ref, v_ref, probs_ref, hgain_ref, cos_ref, sin_ref,
    dz_ref, part_ref, dq_ref, term_ref,
    w_ref, datt_ref, ds_ref, sem, xsem,
):
    half, head = wm_ref.shape[0], q_ref.shape[1]
    rows, width = dz_ref.shape
    arrived = fetch(
        (own_ref, (b1_ref, b2_ref, b3_ref), (a1_ref, a2_ref, a3_ref)), slot_ref[0], dz_ref, xsem
    )
    low = pltpu.make_async_copy(wm_ref, w_ref.at[pl.ds(0, half)], sem.at[0])
    high = pltpu.make_async_copy(wo_ref, w_ref.at[pl.ds(half, half)], sem.at[1])
    low.start()
    high.start()
    low.wait()
    high.wait()
    arrived()
    datt_ref[...] = mm(dz_ref[...], w_ref[:, 3 * head : 4 * head]).astype(BF16)
    term = jnp.zeros((1, head), F32)
    for r, n in tiles(rows, 128):
        p = probs_ref[pl.ds(r, n), :]
        dp = mm_nt(datt_ref[pl.ds(r, n), :], v_ref[...])
        ds = (p * (dp - jnp.sum(dp * p, axis=-1, keepdims=True))).astype(BF16)
        ds_ref[pl.ds(r, n), :] = ds
        dq = (mm(ds, k_ref[...]) * SCALE).astype(BF16).astype(F32)
        cosine, sine = cos_ref[pl.ds(r, n), :], sin_ref[pl.ds(r, n), :]
        e = rotate_back(dq, cosine, sine)
        raw = qraw_ref[pl.ds(r, n), :]
        term = term + norm_term(raw, e)
        dq_ref[pl.ds(r, n), :] = norm_back(raw, e, hgain_ref[4:5, :]).astype(BF16)
    term_ref[...] = term
    part_ref[:, :width] = mm_nt(dq_ref[...], w_ref[:, :head]).astype(BF16)
    part_ref[:, width : width + head] = (mm_tn(ds_ref[...], q_ref[...]) * SCALE).astype(BF16)
    part_ref[:, width + head :] = mm_tn(probs_ref[...].astype(BF16), datt_ref[...]).astype(BF16)


def last_rows(
    g_ref, xp_ref, xn1_ref, dh_ref, kraw_ref, cos_ref, sin_ref, hgain_ref, gains_ref, order_ref,
    pick_ref, slot_ref, t1_ref, t2_ref, t3_ref, qterm_ref, wm_ref, wo_ref,
    out_ref, own_ref, other_ref,
    w_ref, sem,
):
    half, head = wm_ref.shape[0], kraw_ref.shape[1]
    n, width = dh_ref.shape
    low = pltpu.make_async_copy(wm_ref, w_ref.at[pl.ds(0, half)], sem.at[0])
    high = pltpu.make_async_copy(wo_ref, w_ref.at[pl.ds(half, half)], sem.at[1])
    low.start()
    high.start()
    here = pl.ds(pl.multiple_of(slot_ref[0] * n, n), n)
    joined = total(g_ref)
    dk = joined[:, width : width + head].astype(BF16).astype(F32)
    e = rotate_back(dk, cos_ref[here, :], sin_ref[here, :])
    raw = kraw_ref[here, :]
    kterm = norm_term(raw, e)
    dkr = norm_back(raw, e, hgain_ref[5:6, :]).astype(BF16)
    dkv = jnp.concatenate([dkr, joined[:, width + head :].astype(BF16)], axis=1)
    low.wait()
    high.wait()
    dxn1 = joined[:, :width] + mm_nt(dkv, w_ref[:, head : 3 * head])
    x = xp_ref[here, :].astype(F32)
    dx = (dh_ref[...] + norm_back(x, dxn1, gains_ref[0:1, :])).astype(BF16)
    term = norm_term(x, dxn1)
    choose = one_hot(order_ref, width)
    out_ref[...] = mm_nt(dx, choose).astype(BF16)
    grad = mm_tn(xn1_ref[here, :], dkv)
    own_ref[:, : 2 * head] = grad[:half].astype(BF16)
    other_ref[:, : 2 * head] = grad[half:].astype(BF16)
    small = jnp.concatenate([qterm_ref[...], kterm, jnp.zeros((6, head), F32)], axis=0)
    small = mm_nt(small.astype(BF16), one_hot(pick_ref, width))
    terms = [term, t1_ref[...], t2_ref[...], t3_ref[...], small[0:2], jnp.zeros((122, width), F32)]
    terms = jnp.concatenate(terms, axis=0).T
    own_ref[:, 2 * head :] = terms[:half].astype(BF16)
    other_ref[:, 2 * head :] = terms[half:].astype(BF16)


def rope_tables(place, width):
    half = width // 2
    expo = jnp.arange(half, dtype=jnp.float32) * (-2.0 / width)
    freqs = jnp.exp(expo * LOGBASE)
    angle = place.astype(jnp.float32)[:, None] * freqs[None, :]
    return (jnp.cos(angle), jnp.sin(angle))


def bucket_layout(lengths, rows):
    position = jnp.arange(rows, dtype=jnp.int32)
    first = lengths[0]
    ends = lengths[0] + lengths[1]
    segment = jnp.where(position < first, 0, jnp.where(position < ends, 1, 2)).astype(jnp.int32)
    begin = jnp.where(segment == 0, 0, jnp.where(segment == 1, first, ends))
    return (segment, position - begin)


def on_device(
    tokens,
    cotangent,
    seq_lengths,
    query_weight,
    key_weight,
    value_weight,
    outproj_weight,
    gate_weight,
    up_weight,
    down_weight,
    attn_gain,
    attnout_gain,
    ffn_gain,
    ffnout_gain,
    query_gain,
    key_gain,
):
    width = tokens.shape[3]
    wide, narrow = lax.axis_size("wide"), lax.axis_size("narrow")
    chips = wide // 2
    core = lax.axis_index("wide") % 2
    slot = lax.axis_index("narrow")
    slots = jnp.reshape(slot, (1,)).astype(jnp.int32)
    same_core = [[i for i in range(wide) if i % 2 == c] for c in range(2)]
    swap = [(i, i ^ 1) for i in range(wide)]
    upward = [(i, i + 1) for i in range(narrow - 1)]
    downward = [(i + 1, i) for i in range(narrow - 1)]
    dw = width // wide
    dh = query_gain.shape[0]
    head = key_weight.shape[1]
    units = gate_weight.shape[1]
    half = width // 2

    j = jnp.arange(width, dtype=jnp.int32)
    chip, side, rest = (j % half) // dw, j // half, j % dw
    order = ((2 * chip + (core + side) % 2) * dw + rest)[None, :]

    def gather_wide(value, axis):
        return lax.all_gather(
            value, "wide", axis=axis, tiled=True, axis_index_groups=same_core
        )

    def sibling(value):
        return lax.ppermute(value, "wide", swap)

    def pair_sum(own, other):
        return (own.astype(F32) + sibling(other).astype(F32)).astype(BF16)

    def scatter_wide(value, axis):
        return lax.psum_scatter(
            value, "wide", scatter_dimension=axis, tiled=True, axis_index_groups=same_core
        )

    def after(value, *others):
        return lax.optimization_barrier((value, *others))[0]

    def gather_z(value, hook=None):
        up = down = value
        below, above = [], []
        for s in range(1, narrow):
            up = lax.ppermute(up, "narrow", upward)
            down = lax.ppermute(down, "narrow", downward)
            below.append(up)
            above.append(down)
            if hook is not None:
                hook((up, down), s)
        return [value] + below + above

    def exchange_z(value):
        parts = value.reshape(narrow, -1, value.shape[1])
        return lax.all_to_all(parts, "narrow", split_axis=0, concat_axis=0, tiled=True)

    def enter(value):
        value = value.reshape(value.shape[0], value.shape[2], width)
        value = lax.all_to_all(value, "wide", split_axis=0, concat_axis=0, tiled=True)
        return value.reshape(-1, width)

    def leave(value):
        value = value.reshape(wide, -1, width)
        value = lax.all_to_all(value, "wide", split_axis=0, concat_axis=0, tiled=True)
        return value.reshape(wide, 1, -1, width)

    bf, ff = BF16, F32
    pack = call(packing, [((dw, 4 * head + 128), bf)], count=10, flops=10**6, moved=10**6)(
        query_weight, key_weight, value_weight, outproj_weight,
        attn_gain, attnout_gain, ffn_gain, ffnout_gain, query_gain, key_gain,
    )[0]
    own_x = enter(tokens)
    quarter = own_x.shape[0]
    rows = quarter * narrow
    wa_mine = gather_wide(pack, 0)
    held = {}

    def swap_attention(piece, step):
        if step == 1:
            parts = after(jnp.stack([gate_weight, up_weight, down_weight]), *piece)
            held["wf"] = gather_wide(parts, 1)
        if step == narrow - 1:
            held["wa"] = sibling(after(wa_mine, *piece))

    x_all = gather_z(own_x, swap_attention)
    wa_other, wf_mine = held["wa"], held["wf"]
    own_dy = enter(after(cotangent, own_x))
    segment, place = bucket_layout(seq_lengths[0], rows)
    cosine, sine = rope_tables(place, head)
    valid = lax.dynamic_slice_in_dim((segment < 2).astype(F32), slot * quarter, quarter)[:, None]
    t = jnp.arange(head, dtype=jnp.int32)
    owner = t // dh
    pick = (((owner % 2 + core) % 2) * half + (owner // 2) * dw + t % dh)[None, :]

    w_scratch = pltpu.VMEM((width, wa_mine.shape[1]), bf)
    f_scratch = pltpu.VMEM((3, width, units), bf)
    sem = pltpu.SemaphoreType.DMA
    xsem = sem((2 * narrow - 1,))
    seven = tuple(range(2 * narrow - 1))
    k0 = len(seven)
    xp, xn1, qraw, kraw, q, k, v, probs, attended, z_part, gains, hgain = call(
        attention_forward,
        [
            ((rows, width), bf), ((rows, width), bf), ((rows, head), ff), ((rows, head), ff),
            ((rows, head), bf), ((rows, head), bf), ((rows, head), bf), ((rows, rows), ff),
            ((rows, head), bf), ((rows, width), bf), ((8, width), ff), ((8, head), ff),
        ],
        scratch=[pltpu.VMEM((rows, width), bf), w_scratch, sem((2,)), xsem],
        anys=seven + (k0 + 2, k0 + 3), smem=(k0 + 8,), count=k0 + 9, flops=3 * 10**9, moved=8 * 10**6,
    )(*x_all, order, pick, wa_mine, wa_other, cosine, sine, segment[:, None], segment[None, :], slots)
    z = exchange_z(z_part)
    mixed, h, xn2_own = call(
        middle_forward,
        [((quarter, width), ff), ((quarter, width), ff), ((quarter, width), bf)],
        smem=(3,), count=4, flops=10**7, moved=3 * 10**6,
    )(z, xp, gains, slots)
    def swap_ffn(piece, step):
        if step == narrow - 2:
            held["wf"] = sibling(after(wf_mine, *piece))

    xn2_all = gather_z(xn2_own, swap_ffn)
    wf_other = held["wf"]
    xn2, act, fa, fb, m_part = call(
        ffn_forward,
        [((rows, width), bf)] + [((rows, units), bf)] * 3 + [((rows, width), bf)],
        scratch=[f_scratch, sem((6,)), xsem],
        anys=seven + (k0, k0 + 1), smem=(k0 + 2,), count=k0 + 3, flops=6 * 10**9, moved=20 * 10**6,
    )(*xn2_all, wf_mine, wf_other, slots)
    m = exchange_z(m_part)
    out_own, d_out, dm_own, ffnout_term = call(
        middle_turn,
        [((quarter, width), bf), ((quarter, width), ff), ((quarter, width), bf), ((1, width), ff)],
        count=6, flops=10**8, moved=4 * 10**6,
    )(m, h, own_dy, order, valid, gains)
    dm_all = gather_z(dm_own)
    dm, d_gate, d_up, dxn2_part = call(
        ffn_backward,
        [((rows, width), bf)] + [((rows, units), bf)] * 2 + [((rows, width), bf)],
        scratch=[f_scratch, sem((6,)), xsem],
        anys=seven + (k0 + 2, k0 + 3), smem=(k0 + 4,), count=k0 + 5, flops=6 * 10**9, moved=20 * 10**6,
    )(*dm_all, fa, fb, wf_mine, wf_other, slots)
    dxn2 = lax.psum_scatter(
        dxn2_part.reshape(narrow, quarter, width), "narrow", scatter_dimension=0, tiled=True
    )

    def outer(left, right):
        own, other = call(
            weight_grad,
            [((half, right.shape[1]), bf)] * 2,
            scratch=[pltpu.VMEM((width, left.shape[0]), bf)],
            count=2, flops=2 * width * left.shape[0] * right.shape[1], moved=8 * 10**6,
        )(left, right)
        return own, other

    ffn_own, ffn_other = call(
        ffn_weight_grads,
        [((3, half, units), bf)] * 2,
        scratch=[pltpu.VMEM((width, rows), bf), sem((2,))],
        count=5, flops=10**6, moved=10**6,
    )(dm, xn2, act, d_gate, d_up)
    ffn_sum = pair_sum(ffn_own, ffn_other)
    dxn2 = after(dxn2, ffn_sum)
    s_ffn = scatter_wide(ffn_sum, 1)
    left_out = leave(out_own)
    d_resid, dz_own, ffn_term, attnout_term = call(
        middle_backward,
        [((quarter, width), ff), ((quarter, width), bf), ((1, width), ff), ((1, width), ff)],
        count=5, flops=10**7, moved=4 * 10**6,
    )(dxn2, d_out, h, mixed, gains)
    dz_all = gather_z(dz_own)
    dz, joined_part, dq_raw, query_term = call(
        attention_backward,
        [((rows, width), bf), ((rows, width + 2 * head), bf), ((rows, head), bf), ((1, head), ff)],
        scratch=[
            w_scratch, pltpu.VMEM((rows, head), bf), pltpu.VMEM((rows, rows), bf), sem((2,)), xsem,
        ],
        smem=(k0,), anys=seven + (k0 + 1, k0 + 2), count=k0 + 11, flops=3 * 10**9, moved=8 * 10**6,
    )(*dz_all, slots, wa_mine, wa_other, qraw, q, k, v, probs, hgain, cosine, sine)
    joined = exchange_z(joined_part)
    g_outproj = outer(dz, attended)
    g_query = outer(xn1, dq_raw)
    s_ffn = s_ffn.astype(F32)
    joined = after(joined, left_out, s_ffn, *g_outproj, *g_query)
    s_outproj = scatter_wide(pair_sum(*g_outproj), 0)
    dx_own, own, other = call(
        last_rows,
        [((quarter, width), bf)] + [((half, 2 * head + 128), bf)] * 2,
        scratch=[w_scratch, sem((2,))],
        smem=(11,), anys=(16, 17), count=18, flops=10**9, moved=8 * 10**6,
    )(
        joined, xp, xn1, d_resid, kraw, cosine, sine, hgain, gains, order, pick, slots,
        attnout_term, ffn_term, ffnout_term, query_term, wa_mine, wa_other,
    )
    s_query = scatter_wide(pair_sum(*g_query), 0)
    last = scatter_wide(pair_sum(own, other), 0)
    shared = lax.all_gather(last, "narrow").astype(F32).sum(axis=0)
    small = shared[:, 2 * head :]
    return (
        left_out,
        leave(dx_own),
        s_query.astype(F32),
        shared[:, :head],
        shared[:, head : 2 * head],
        s_outproj.astype(F32),
        s_ffn[0],
        s_ffn[1],
        s_ffn[2],
        small[:, 0],
        small[:, 1],
        small[:, 2],
        small[:, 3],
        small[:dh, 4],
        small[:dh, 5],
    )


def solution(mesh):
    return jax.shard_map(
        on_device,
        mesh=mesh,
        in_specs=(
            P(None, "narrow", "wide", None),
            P(None, "narrow", "wide", None),
            P("wide", None),
            P("wide", "narrow"),
            P("wide", None),
            P("wide", None),
            P("wide", "narrow"),
            P("wide", "narrow"),
            P("wide", "narrow"),
            P("wide", "narrow"),
            P("wide"),
            P("wide"),
            P("wide"),
            P("wide"),
            P("wide"),
            P("wide"),
        ),
        out_specs=(
            P(None, "narrow", "wide", None),
            P(None, "narrow", "wide", None),
            P("wide", "narrow"),
            P("wide", None),
            P("wide", None),
            P("wide", "narrow"),
            P("wide", "narrow"),
            P("wide", "narrow"),
            P("wide", "narrow"),
            P("wide"),
            P("wide"),
            P("wide"),
            P("wide"),
            P("wide"),
            P("wide"),
        ),
        check_vma=False,
    )
```

```python
import functools
import math

import jax
import jax.numpy as jnp
from jax import lax
from jax.experimental import pallas as pl
from jax.experimental.pallas import tpu as pltpu
from jax.sharding import PartitionSpec as P

EPS = 1e-06
SCALE = 0.0625
LOGBASE = math.log(1000000.0)
GELU_C = 0.7978845608028654
GELU_A = 0.044715
F32, BF16 = jnp.float32, jnp.bfloat16
VMEM_LIMIT = 60 * 1024 * 1024
CHUNKS = 1
RING = 4


def call(kernel, outs, scratch=(), anys=(), smem=(), count=0, flops=0, moved=0):
    def place(index):
        if index in anys:
            return pl.BlockSpec(memory_space=pl.ANY)
        if index in smem:
            return pl.BlockSpec(memory_space=pltpu.SMEM)
        return pl.BlockSpec(memory_space=pltpu.VMEM)

    return pl.pallas_call(
        kernel,
        out_shape=[jax.ShapeDtypeStruct(s, d) for s, d in outs],
        in_specs=[place(i) for i in range(count)],
        out_specs=[pl.BlockSpec(memory_space=pltpu.VMEM)] * len(outs),
        scratch_shapes=list(scratch),
        compiler_params=pltpu.CompilerParams(vmem_limit_bytes=VMEM_LIMIT),
        cost_estimate=pl.CostEstimate(flops=1, bytes_accessed=1, transcendentals=0),
    )


def mm(a, b):
    return lax.dot_general(a, b, (((1,), (0,)), ((), ())), preferred_element_type=F32)


def mm_nt(a, b):
    return lax.dot_general(a, b, (((1,), (1,)), ((), ())), preferred_element_type=F32)


def mm_tn(a, b):
    return lax.dot_general(a, b, (((0,), (0,)), ((), ())), preferred_element_type=F32)


def root(v):
    return lax.rsqrt(jnp.mean(v * v, axis=-1, keepdims=True) + EPS)


def norm(v, gain):
    return v * root(v) * (1.0 + gain)


def norm_back(v, grad, gain):
    r = root(v)
    e = grad * (1.0 + gain)
    return r * e - v * (r * r * r * jnp.mean(e * v, axis=-1, keepdims=True))


def norm_term(v, grad):
    return jnp.sum(grad * v * root(v), axis=0, keepdims=True)


def rotate(v, cosine, sine):
    half = v.shape[-1] // 2
    a, b = v[:, :half], v[:, half:]
    return jnp.concatenate([a * cosine - b * sine, b * cosine + a * sine], axis=-1)


def rotate_back(v, cosine, sine):
    half = v.shape[-1] // 2
    a, b = v[:, :half], v[:, half:]
    return jnp.concatenate([a * cosine + b * sine, b * cosine - a * sine], axis=-1)


def tiles(extent, size):
    return [(i, min(size, extent - i)) for i in range(0, extent, size)]


def packing(q_ref, k_ref, v_ref, o_ref, g0_ref, g1_ref, g2_ref, g3_ref, g4_ref, g5_ref, out_ref):
    rows, head = q_ref.shape
    for i, ref in enumerate((q_ref, k_ref, v_ref, o_ref)):
        out_ref[:, i * head : (i + 1) * head] = ref[...]
    lane = lax.broadcasted_iota(jnp.int32, (rows, 128), 1)
    columns = jnp.zeros((rows, 128), F32)
    for i, ref in enumerate((g0_ref, g1_ref, g2_ref, g3_ref, g4_ref, g5_ref)):
        n = ref.shape[0]
        same = lax.broadcasted_iota(jnp.int32, (rows, n), 0) == lax.broadcasted_iota(
            jnp.int32, (rows, n), 1
        )
        column = jnp.sum(jnp.where(same, ref[...].astype(F32)[None, :], 0.0), axis=1, keepdims=True)
        columns = jnp.where(lane == i, column, columns)
    out_ref[:, 4 * head :] = columns.astype(BF16)


def one_hot(order, rows):
    index = lax.broadcasted_iota(jnp.int32, (rows, order.shape[1]), 0)
    return jnp.where(index == order, 1.0, 0.0).astype(BF16)


def steps(value, size, count):
    return sum(jnp.where(value >= size * i, 1, 0) for i in range(1, count))


def orders(core, width, head, wide):
    half, dw, dh = width // 2, width // wide, head // wide
    place = lax.broadcasted_iota(jnp.int32, (1, width), 1)
    side = jnp.where(place >= half, 1, 0)
    inner = place - half * side
    chip = steps(inner, dw, wide // 2)
    order = (2 * chip + ((core + side) & 1)) * dw + (inner - chip * dw)
    entry = lax.broadcasted_iota(jnp.int32, (1, head), 1)
    owner = steps(entry, dh, wide)
    chip = steps(owner, 2, wide // 2)
    pick = (((owner & 1) + core) & 1) * half + chip * dw + (entry - owner * dh)
    return order, pick


def segments(position, first, ends):
    segment = jnp.where(position < first, 0, jnp.where(position < ends, 1, 2))
    begin = jnp.where(position < first, 0, jnp.where(position < ends, first, ends))
    return segment, position - begin


def attention_forward(wide, *refs):
    x_refs, weight_refs, info_ref, refs = refs[:RING], refs[RING:-26], refs[-26], refs[-25:]
    (
        xp_ref, xn1_ref, qraw_ref, kraw_ref, q_ref, k_ref, v_ref, probs_ref, att_ref, gains_ref,
        hgain_ref, wkv_ref, wout_ref, cos_ref, sin_ref, order_ref, pick_ref, *part_refs,
        part_ref, x_ref, w_ref, sem,
    ) = refs
    head = q_ref.shape[1]
    rows, width = x_ref.shape
    half = width // 2
    slot, core, first, ends = info_ref[0], info_ref[1], info_ref[2], info_ref[3]
    copies, count = [], len(weight_refs) // 2
    for i, ref in enumerate(weight_refs):
        n = ref.shape[0]
        at = pl.multiple_of(info_ref[4 + i % count] * n + half * (1 - i // count), 16)
        copies.append(pltpu.make_async_copy(ref, w_ref.at[pl.ds(at, n)], sem.at[i]))
        copies[-1].start()
    collect(x_refs, slot, x_ref)
    order, pick = orders(core, width, head, wide)
    order_ref[...] = order
    pick_ref[...] = pick
    choose = one_hot(order, width)
    step = 128
    for r, n in tiles(rows, step):
        xp_ref[pl.ds(r, n), :] = mm(x_ref[pl.ds(r, n), :], choose).astype(BF16)
    frequency = jnp.exp(
        lax.broadcasted_iota(jnp.int32, (1, head // 2), 1).astype(F32) * (-2.0 / head) * LOGBASE
    )
    for r, n in tiles(rows, step):
        position = lax.broadcasted_iota(jnp.int32, (n, 1), 0) + r
        angle = segments(position, first, ends)[1].astype(F32) * frequency
        cos_ref[pl.ds(r, n), :] = jnp.cos(angle)
        sin_ref[pl.ds(r, n), :] = jnp.sin(angle)
    for c in copies:
        c.wait()
    columns = w_ref[:, 4 * head :].T
    gains_ref[...] = columns[:8].astype(F32)
    hgain_ref[...] = mm(columns[:8], one_hot(pick, width))
    wkv_ref[...] = w_ref[:, head : 3 * head]
    wout_ref[...] = w_ref[:, 3 * head : 4 * head]
    for r, n in tiles(rows, step):
        x = xp_ref[pl.ds(r, n), :].astype(F32)
        xn1_ref[pl.ds(r, n), :] = norm(x, gains_ref[0:1, :]).astype(BF16)
    gq, gk = hgain_ref[4:5, :], hgain_ref[5:6, :]
    raw = mm(xn1_ref[...], w_ref[:, : 3 * head])
    qraw_ref[...] = raw[:, :head]
    kraw_ref[...] = raw[:, head : 2 * head]
    v_ref[...] = raw[:, 2 * head :].astype(BF16)
    cosine, sine = cos_ref[...], sin_ref[...]
    q_ref[...] = rotate(norm(raw[:, :head], gq), cosine, sine).astype(BF16)
    k_ref[...] = rotate(norm(raw[:, head : 2 * head], gk), cosine, sine).astype(BF16)
    for r, n in tiles(rows, step):
        s = mm_nt(q_ref[pl.ds(r, n), :], k_ref[...]) * SCALE
        row = lax.broadcasted_iota(jnp.int32, s.shape, 0) + r
        col = lax.broadcasted_iota(jnp.int32, s.shape, 1)
        keep = (segments(row, first, ends)[0] == segments(col, first, ends)[0]) & (col <= row)
        s = jnp.where(keep, s, -1e30)
        e = jnp.exp(s - jnp.max(s, axis=-1, keepdims=True))
        p = e / jnp.sum(e, axis=-1, keepdims=True)
        probs_ref[pl.ds(r, n), :] = p
        att_ref[pl.ds(r, n), :] = mm(p.astype(BF16), v_ref[...]).astype(BF16)
    for r, n in tiles(rows, step):
        part_ref[pl.ds(r, n), :] = mm_nt(
            att_ref[pl.ds(r, n), :], w_ref[:, 3 * head : 4 * head]
        ).astype(BF16)
    hand_out(part_ref, slot, part_refs)


def hand_out(whole_ref, slot, refs):
    for s, ref in enumerate(refs):
        n = ref.shape[0]
        at = lax.rem(slot + s, len(refs)) * n
        ref[...] = whole_ref[pl.ds(pl.multiple_of(at, n), n), :]


def spread(whole_ref, refs):
    for s, ref in enumerate(refs):
        n = ref.shape[0]
        ref[...] = whole_ref[pl.ds((len(refs) - s) % len(refs) * n, n), :]


def collect(refs, slot, target):
    for s, ref in enumerate(refs):
        n = ref.shape[0]
        at = pl.multiple_of(lax.rem(slot + len(refs) - s, len(refs)) * n, n)
        target[pl.ds(at, n), :] = ref[...]


def total(refs):
    out = refs[0][...].astype(F32)
    for ref in refs[1:]:
        out = out + ref[...].astype(F32)
    return out


def middle_forward(*refs):
    *z_refs, xp_ref, gains_ref, slot_ref, mixed_ref, h_ref = refs[:-CHUNKS]
    n = h_ref.shape[0]
    x = xp_ref[pl.ds(pl.multiple_of(slot_ref[0] * n, n), n), :].astype(F32)
    z = total(z_refs)
    h = x + norm(z, gains_ref[1:2, :])
    mixed_ref[...] = z
    h_ref[...] = h
    xn2 = norm(h, gains_ref[2:3, :]).astype(BF16)
    for c, ref in enumerate(refs[-CHUNKS:]):
        ref[...] = xn2[c * ref.shape[0] : (c + 1) * ref.shape[0]]


def load_weights(sources, target, sem, order):
    half = sources[0].shape[1]
    waits = []
    for i in order:
        pair = [
            pltpu.make_async_copy(
                ref.at[i], target.at[i, pl.ds(j * half, half)], sem.at[2 * i + j]
            )
            for j, ref in enumerate(sources)
        ]
        for c in pair:
            c.start()
        waits.append(lambda pair=pair: [c.wait() for c in pair])
    return waits


def ffn_forward(*refs):
    wm_ref, wo_ref = refs[RING : RING + 2]
    x_ref, act_ref, fa_ref, fb_ref, *part_refs = refs[RING + 2 : -3]
    part_ref, w_ref, sem = refs[-3:]
    waits = load_weights((wm_ref, wo_ref), w_ref, sem, (0, 1, 2))
    for s in range(RING):
        n = refs[s].shape[0]
        x_ref[s * n : (s + 1) * n] = refs[s][...]
    waits[0]()
    waits[1]()
    x = x_ref[...]
    for f, n in tiles(act_ref.shape[1], 256):
        gate = mm(x, w_ref[0, :, pl.ds(f, n)])
        up = mm(x, w_ref[1, :, pl.ds(f, n)])
        square = gate * gate
        t = jnp.tanh(GELU_C * (gate + GELU_A * (gate * square)))
        bell = 0.5 * (1.0 + t)
        g = gate * bell
        slope = bell + 0.5 * gate * (1.0 - t * t) * (GELU_C * (1.0 + 3.0 * GELU_A * square))
        act_ref[:, pl.ds(f, n)] = (g * up).astype(BF16)
        fa_ref[:, pl.ds(f, n)] = (slope * up).astype(BF16)
        fb_ref[:, pl.ds(f, n)] = g.astype(BF16)
    waits[2]()
    for d, n in tiles(part_ref.shape[1], 384):
        part_ref[:, pl.ds(d, n)] = mm_nt(act_ref[...], w_ref[2, pl.ds(d, n), :]).astype(BF16)
    spread(part_ref, part_refs)


def middle_turn(chunk, *refs):
    *m_refs, h_ref, dy_ref, order_ref, info_ref, gains_ref = refs[:-4]
    out_ref, dout_ref, dm_ref, term_ref = refs[-4:]
    n = dm_ref.shape[0]
    choose = one_hot(order_ref[...], h_ref.shape[1])
    m = total(m_refs)
    gain = gains_ref[3:4, :]
    here = pl.ds(chunk * n, n)
    out = (h_ref[here, :] + norm(m, gain)).astype(BF16)
    out_ref[...] = mm_nt(out, choose).astype(BF16)
    position = lax.broadcasted_iota(jnp.int32, (n, 1), 0) + (info_ref[0] * CHUNKS + chunk) * n
    dy = mm(dy_ref[here, :], choose) * jnp.where(position < info_ref[3], 1.0, 0.0)
    dout_ref[...] = dy
    dm_ref[...] = norm_back(m, dy, gain).astype(BF16)
    term_ref[...] = norm_term(m, dy)


def ffn_backward(*refs):
    fa_ref, fb_ref, wm_ref, wo_ref = refs[RING : RING + 4]
    slot_ref, dm_ref, dg_ref, du_ref, part_ref, w_ref, sem = refs[RING + 4 :]
    waits = load_weights((wm_ref, wo_ref), w_ref, sem, (2, 0, 1))
    for s in range(RING):
        n = refs[s].shape[0]
        dm_ref[s * n : (s + 1) * n] = refs[s][...]
    waits[0]()
    dm = dm_ref[...]
    for f, n in tiles(dg_ref.shape[1], 256):
        d = mm(dm, w_ref[2, :, pl.ds(f, n)])
        dg_ref[:, pl.ds(f, n)] = (d * fa_ref[:, pl.ds(f, n)].astype(F32)).astype(BF16)
        du_ref[:, pl.ds(f, n)] = (d * fb_ref[:, pl.ds(f, n)].astype(F32)).astype(BF16)
    waits[1]()
    waits[2]()
    for d, n in tiles(part_ref.shape[1], 384):
        part = mm_nt(dg_ref[...], w_ref[0, pl.ds(d, n), :])
        part = (part + mm_nt(du_ref[...], w_ref[1, pl.ds(d, n), :])).astype(BF16)
        for s in range(RING):
            m = refs[s].shape[0]
            at = pl.multiple_of(lax.rem(slot_ref[0] + RING - s, RING) * m, m)
            part_ref[pl.ds(at, m), pl.ds(d, n)] = part[s * m : (s + 1) * m]


def weight_grad(left_ref, right_ref, own_ref, other_ref, turned_ref):
    turned_ref[...] = left_ref[...].T
    half, n_right = own_ref.shape
    for r, n in tiles(half, 192):
        for at, out in ((r, own_ref), (half + r, other_ref)):
            grad = mm(turned_ref[pl.ds(at, n), :], right_ref[:, :n_right])
            out[pl.ds(r, n), :] = grad.astype(BF16)


def ffn_weight_grads(first, *refs):
    groups = [refs[CHUNKS * i : CHUNKS * (i + 1)] for i in range(5)]
    dm, xn2, act, dg, du = groups
    *rest, turned_ref = refs[CHUNKS * 5 :]
    half, part = turned_ref.shape[0], dm[0].shape[0]
    received = rest[:3] if len(rest) == 4 else []
    outs = [rest[3].at[i] for i in range(3)] if received else rest
    for i, (left, right) in enumerate(((xn2, dg), (xn2, du), (dm, act))):
        if i != 1:
            for c, ref in enumerate(left):
                turned = ref[:, first : first + half].T
                turned_ref[:, c * part : (c + 1) * part] = turned
        for r, n in tiles(half, 192):
            grad = sum(
                mm(turned_ref[pl.ds(r, n), c * part : (c + 1) * part], right[c][...])
                for c in range(CHUNKS)
            )
            if received:
                grad = grad + received[i][pl.ds(r, n), :].astype(F32)
            outs[i][pl.ds(r, n), :] = grad.astype(BF16)


def load_heads(sources, target, sem):
    half = sources[0].shape[1]
    copies = [
        pltpu.make_async_copy(
            ref, target.at[:, pl.ds(j * half, half), :], sem.at[j]
        )
        for j, ref in enumerate(sources)
    ]
    for c in copies:
        c.start()
    return lambda: [c.wait() for c in copies]


def middle_backward(g_ref, dout_ref, h_ref, mixed_ref, gains_ref, dh_ref, dz_ref, fterm_ref, aterm_ref):
    dxn2 = g_ref[0].astype(F32)
    h, mixed = h_ref[...], mixed_ref[...]
    dh = dout_ref[...] + norm_back(h, dxn2, gains_ref[2:3, :])
    dh_ref[...] = dh
    dz_ref[...] = norm_back(mixed, dh, gains_ref[1:2, :]).astype(BF16)
    fterm_ref[...] = norm_term(h, dxn2)
    aterm_ref[...] = norm_term(mixed, dh)


def attention_backward(*refs):
    (
        slot_ref, wout_ref, qraw_ref, q_ref, k_ref, v_ref, probs_ref, hgain_ref, cos_ref, sin_ref,
        dz_ref, part_ref, term_ref, *out_refs, datt_ref, ds_ref,
    ) = refs[RING:]
    rows, head = q_ref.shape
    collect(refs[:RING], slot_ref[0], dz_ref)
    datt_ref[...] = mm(dz_ref[...], wout_ref[...]).astype(BF16)
    term = jnp.zeros((1, head), F32)
    for r, n in tiles(rows, 128):
        p = probs_ref[pl.ds(r, n), :]
        dp = mm_nt(datt_ref[pl.ds(r, n), :], v_ref[...])
        ds = (p * (dp - jnp.sum(dp * p, axis=-1, keepdims=True))).astype(BF16)
        ds_ref[pl.ds(r, n), :] = ds
        dq = (mm(ds, k_ref[...]) * SCALE).astype(BF16).astype(F32)
        cosine, sine = cos_ref[pl.ds(r, n), :], sin_ref[pl.ds(r, n), :]
        e = rotate_back(dq, cosine, sine)
        raw = qraw_ref[pl.ds(r, n), :]
        term = term + norm_term(raw, e)
        part_ref[pl.ds(r, n), :head] = norm_back(raw, e, hgain_ref[4:5, :]).astype(BF16)
    term_ref[...] = term
    part_ref[:, head : 2 * head] = (mm_tn(ds_ref[...], q_ref[...]) * SCALE).astype(BF16)
    part_ref[:, 2 * head :] = mm_tn(probs_ref[...].astype(BF16), datt_ref[...]).astype(BF16)
    hand_out(part_ref, slot_ref[0], out_refs)


def last_rows(
    g0_ref, g1_ref, g2_ref, g3_ref, xp_ref, xn1_ref, dh_ref, kraw_ref, cos_ref, sin_ref, hgain_ref, gains_ref, order_ref,
    pick_ref, slot_ref, t1_ref, t2_ref, t3_ref, qterm_ref, qm_ref, qo_ref, om_ref, oo_ref, w_ref, hm_ref, ho_ref,
    out_ref, own_ref, other_ref,
    wq_ref, hsem,
):
    head = kraw_ref.shape[1]
    n, width = dh_ref.shape
    half = width // 2
    arrived = load_heads((hm_ref, ho_ref), wq_ref, hsem)
    here = pl.ds(pl.multiple_of(slot_ref[0] * n, n), n)
    g_refs = (g0_ref, g1_ref, g2_ref, g3_ref)
    joined = sum(ref[:, head:].astype(F32) for ref in g_refs)
    dk = joined[:, :head].astype(BF16).astype(F32)
    e = rotate_back(dk, cos_ref[here, :], sin_ref[here, :])
    raw = kraw_ref[here, :]
    kterm = norm_term(raw, e)
    dkr = norm_back(raw, e, hgain_ref[5:6, :]).astype(BF16)
    dkv = jnp.concatenate([dkr, joined[:, head:].astype(BF16)], axis=1)
    dxn1 = mm_nt(dkv, w_ref[...])
    arrived()
    for i, ref in enumerate(g_refs):
        dxn1 = dxn1 + mm_nt(ref[:, :head], wq_ref[i])
    x = xp_ref[here, :].astype(F32)
    dx = (dh_ref[...] + norm_back(x, dxn1, gains_ref[0:1, :])).astype(BF16)
    term = norm_term(x, dxn1)
    choose = one_hot(order_ref[...], width)
    out_ref[...] = mm_nt(dx, choose).astype(BF16)
    grad = mm_tn(xn1_ref[here, :], dkv)
    for i, (mine, others) in enumerate(((qm_ref, qo_ref), (om_ref, oo_ref))):
        own_ref[:, i * head : (i + 1) * head] = mine[...]
        other_ref[:, i * head : (i + 1) * head] = others[...]
    own_ref[:, 2 * head : 4 * head] = grad[:half].astype(BF16)
    other_ref[:, 2 * head : 4 * head] = grad[half:].astype(BF16)
    small = jnp.concatenate([qterm_ref[...], kterm, jnp.zeros((6, head), F32)], axis=0)
    small = mm_nt(small.astype(BF16), one_hot(pick_ref[...], width))
    terms = [term, t1_ref[...], t2_ref[...], t3_ref[...], small[0:2], jnp.zeros((122, width), F32)]
    terms = jnp.concatenate(terms, axis=0).T
    own_ref[:, 4 * head :] = terms[:half].astype(BF16)
    other_ref[:, 4 * head :] = terms[half:].astype(BF16)


def on_device(
    tokens,
    cotangent,
    seq_lengths,
    query_weight,
    key_weight,
    value_weight,
    outproj_weight,
    gate_weight,
    up_weight,
    down_weight,
    attn_gain,
    attnout_gain,
    ffn_gain,
    ffnout_gain,
    query_gain,
    key_gain,
):
    width = tokens.shape[3]
    wide, narrow = lax.axis_size("wide"), lax.axis_size("narrow")
    chips = wide // 2
    core = lax.axis_index("wide") % 2
    slot = lax.axis_index("narrow")
    slots = jnp.reshape(slot, (1,)).astype(jnp.int32)
    same_core = [[i for i in range(wide) if i % 2 == c] for c in range(2)]
    swap = [(i, i ^ 1) for i in range(wide)]
    upward = [(i, i + 1) for i in range(narrow - 1)]
    downward = [(i + 1, i) for i in range(narrow - 1)]
    dw = width // wide
    dh = query_gain.shape[0]
    head = key_weight.shape[1]
    units = gate_weight.shape[1]
    half = width // 2

    def gather_wide(value, axis):
        return lax.all_gather(
            value, "wide", axis=axis, tiled=True, axis_index_groups=same_core
        )

    def sibling(value):
        return lax.ppermute(value, "wide", swap)

    def pair_sum(own, other):
        return (own.astype(F32) + sibling(other).astype(F32)).astype(BF16)

    def scatter_wide(value, axis):
        return lax.psum_scatter(
            value, "wide", scatter_dimension=axis, tiled=True, axis_index_groups=same_core
        )

    def after(value, *others):
        return lax.optimization_barrier((value, *others))[0]

    def gather_rows(value):
        return lax.all_gather(value, "narrow", axis=0, tiled=True)

    def gather_ring(value):
        return pass_on([value] * narrow)

    def pass_on(parts):
        got = [parts[0]]
        for s in range(1, narrow):
            shift = [(i, (i + s) % narrow) for i in range(narrow)]
            got.append(lax.ppermute(parts[s], "narrow", shift))
        return got

    def exchange_z(value):
        parts = value.reshape(narrow, -1, value.shape[-1])
        return lax.all_to_all(parts, "narrow", split_axis=0, concat_axis=0, tiled=True)

    def enter(value):
        value = value.reshape(value.shape[0], value.shape[2], width)
        value = lax.all_to_all(value, "wide", split_axis=0, concat_axis=0, tiled=True)
        return value.reshape(-1, width)

    def leave(value):
        value = value.reshape(wide, -1, width)
        value = lax.all_to_all(value, "wide", split_axis=0, concat_axis=0, tiled=True)
        return value.reshape(wide, 1, -1, width)

    bf, ff = BF16, F32
    pack = call(packing, [((dw, 4 * head + 128), bf)], count=10, flops=10**6, moved=10**6)(
        query_weight, key_weight, value_weight, outproj_weight,
        attn_gain, attnout_gain, ffn_gain, ffnout_gain, query_gain, key_gain,
    )[0]
    wa_mine = gather_wide(pack, 0)
    own_x = enter(tokens)
    quarter = own_x.shape[0]
    rows = quarter * narrow
    part = quarter // CHUNKS
    every = range(CHUNKS)
    sem = pltpu.SemaphoreType.DMA
    f_scratch = pltpu.VMEM((3, width, units), bf)
    x_all = gather_ring(own_x)
    wf_mine = gather_wide(after(jnp.stack([gate_weight, up_weight, down_weight]), own_x), 1)
    weights = [sibling(after(wa_mine, *x_all)), wa_mine]
    queries = gather_ring(after(query_weight, *x_all))
    wh_mine = gather_wide(after(jnp.stack(queries), wf_mine), 1)
    lengths = seq_lengths[0]
    info = [slot, core, lengths[0], lengths[0] + lengths[1], 0]
    info = jnp.stack([jnp.asarray(v, jnp.int32) for v in info])
    own_dy = enter(after(cotangent, own_x))
    many = len(x_all) + len(weights)
    (
        xp, xn1, qraw, kraw, q, k, v, probs, attended, gains, hgain, wkv, wout, cosine, sine, order, pick,
        *z_parts,
    ) = call(
        functools.partial(attention_forward, wide),
        [
            ((rows, width), bf), ((rows, width), bf), ((rows, head), ff), ((rows, head), ff),
            ((rows, head), bf), ((rows, head), bf), ((rows, head), bf), ((rows, rows), ff),
            ((rows, head), bf), ((8, width), ff), ((8, head), ff), ((width, 2 * head), bf), ((width, head), bf),
            ((rows, head // 2), ff), ((rows, head // 2), ff), ((1, width), jnp.int32),
            ((1, head), jnp.int32),
        ]
        + [((quarter, width), bf)] * narrow,
        scratch=[
            pltpu.VMEM((rows, width), bf), pltpu.VMEM((rows, width), bf),
            pltpu.VMEM((width, 4 * head + 128), bf), sem((len(weights),)),
        ],
        anys=tuple(range(len(x_all), many)), smem=(many,), count=many + 1,
        flops=3 * 10**9, moved=8 * 10**6,
    )(*x_all, *weights, info)
    z_parts = [after(p, *queries) for p in z_parts]
    z = pass_on(z_parts)
    mixed, h, *xn2_own = call(
        middle_forward,
        [((quarter, width), ff)] * 2 + [((part, width), bf)] * CHUNKS,
        smem=(narrow + 2,), count=narrow + 3, flops=10**7, moved=2 * 10**6,
    )(*z, xp, gains, slots)
    xn2 = [gather_ring(xn2_own[c]) for c in every]
    wf_other = sibling(after(wf_mine, *xn2[0]))
    def ffn_ahead(c):
        return call(
            ffn_forward,
            [((narrow * part, width), bf)] + [((narrow * part, units), bf)] * 3
            + [((part, width), bf)] * narrow,
            scratch=[pltpu.VMEM((narrow * part, width), bf), f_scratch, sem((6,))],
            anys=(narrow, narrow + 1), count=narrow + 2, flops=3 * 10**9, moved=16 * 10**6,
        )(*xn2[c], wf_mine, wf_other)

    ahead = []
    for c in every:
        if c:
            xn2[c][0] = after(xn2[c][0], ahead[-1][1])
        ahead.append(ffn_ahead(c))
    xn2_all, act, fa, fb, *m_part = zip(*ahead)
    m = [pass_on([p[c] for p in m_part]) for c in every]
    out_own, d_out, dm_own, turn_term = zip(*[
        call(
            functools.partial(middle_turn, c),
            [((part, width), bf), ((part, width), ff), ((part, width), bf), ((1, width), ff)],
            smem=(narrow + 3,), count=narrow + 5, flops=10**8, moved=4 * 10**6,
        )(*m[c], h, own_dy, order, info, gains)
        for c in every
    ])
    dm = [gather_ring(dm_own[c]) for c in every]

    dm[0][0] = after(dm[0][0], wh_mine)

    def ffn_back(c):
        return call(
            ffn_backward,
            [((narrow * part, width), bf)] + [((narrow * part, units), bf)] * 2
            + [((narrow * part, width), bf)],
            scratch=[f_scratch, sem((6,))],
            anys=(narrow + 2, narrow + 3), smem=(narrow + 4,), count=narrow + 5,
            flops=3 * 10**9, moved=16 * 10**6,
        )(*dm[c], fa[c], fb[c], wf_mine, wf_other, slots)

    back = []
    for c in every:
        if c:
            dm[c][0] = after(dm[c][0], back[-1][1])
        back.append(ffn_back(c))
    dm_all, d_gate, d_up, dxn2_part = zip(*back)
    dxn2 = lax.psum_scatter(
        dxn2_part[0].reshape(narrow, quarter, width), "narrow", scatter_dimension=0, tiled=True
    )
    saved = (*dm_all, *xn2_all, *act, *d_gate, *d_up)

    def ffn_grads(first, *received):
        outs = [((3, half, units), bf)] if received else [((half, units), bf)] * 3
        return call(
            functools.partial(ffn_weight_grads, first),
            outs,
            scratch=[pltpu.VMEM((half, rows), bf)],
            count=5 * CHUNKS + len(received), flops=10**6, moved=10**6,
        )(*saved, *received)

    ffn_other = [sibling(g) for g in ffn_grads(half)]
    ffn_sum = ffn_grads(0, *ffn_other)[0]
    dxn2 = after(dxn2, ffn_sum)
    s_ffn = scatter_wide(ffn_sum, 1)
    left_out = leave(out_own[0])
    d_resid, dz_own, ffn_term, attnout_term = call(
        middle_backward,
        [((quarter, width), ff), ((quarter, width), bf), ((1, width), ff), ((1, width), ff)],
        count=5, flops=10**7, moved=3 * 10**6,
    )(dxn2, d_out[0], h, mixed, gains)
    dz = gather_ring(dz_own)
    wh_other = sibling(after(wh_mine, dz_own))
    dz_all, joined_part, query_term, *joined = call(
        attention_backward,
        [((rows, width), bf), ((rows, 3 * head), bf), ((1, head), ff)]
        + [((quarter, 3 * head), bf)] * narrow,
        scratch=[pltpu.VMEM((rows, head), bf), pltpu.VMEM((rows, rows), bf)],
        smem=(narrow,), count=narrow + 10, flops=2 * 10**9, moved=6 * 10**6,
    )(*dz, slots, wout, qraw, q, k, v, probs, hgain, cosine, sine)
    joined = pass_on(joined)

    def outer(left, right, columns):
        return call(
            weight_grad,
            [((half, columns), bf)] * 2,
            scratch=[pltpu.VMEM((width, left.shape[0]), bf)],
            count=2, flops=2 * width * left.shape[0] * columns, moved=3 * 10**6,
        )(left, right)

    g_query = outer(xn1, joined_part, head)
    g_outproj = outer(dz_all, attended, head)
    joined[0] = after(joined[0], left_out, *g_query, *g_outproj)
    heads = wh_mine.shape[0]
    dx_own, own, other = call(
        last_rows,
        [((quarter, width), bf)] + [((half, 4 * head + 128), bf)] * 2,
        scratch=[pltpu.VMEM((heads, width, head), bf), sem((2,))],
        smem=(14,), anys=(24, 25), count=26, flops=10**9, moved=8 * 10**6,
    )(
        *joined, xp, xn1, d_resid, kraw, cosine, sine, hgain, gains, order, pick, slots,
        attnout_term, ffn_term, *turn_term, query_term, *g_query, *g_outproj, wkv,
        wh_mine, wh_other,
    )

    def scatter_chips(value):
        parts = value.reshape(chips, dw, value.shape[1])
        parts = lax.all_to_all(
            parts, "wide", split_axis=0, concat_axis=0, tiled=True, axis_index_groups=same_core
        )
        return parts.astype(F32).sum(axis=0)

    left_dx = leave(dx_own)
    last = scatter_chips(after(pair_sum(own, other), left_dx))
    s_query, s_outproj = last[:, :head], last[:, head : 2 * head]
    last = last[:, 2 * head :].astype(BF16)
    last, s_ffn = lax.optimization_barrier((last, s_ffn))
    s_ffn = s_ffn.astype(F32)
    shared = lax.all_gather(last, "narrow").astype(F32).sum(axis=0)
    small = shared[:, 2 * head :]
    return (
        left_out,
        left_dx,
        s_query,
        shared[:, :head],
        shared[:, head : 2 * head],
        s_outproj,
        s_ffn[0],
        s_ffn[1],
        s_ffn[2],
        small[:, 0],
        small[:, 1],
        small[:, 2],
        small[:, 3],
        small[:dh, 4],
        small[:dh, 5],
    )


def solution(mesh):
    return jax.shard_map(
        on_device,
        mesh=mesh,
        in_specs=(
            P(None, "narrow", "wide", None),
            P(None, "narrow", "wide", None),
            P("wide", None),
            P("wide", "narrow"),
            P("wide", None),
            P("wide", None),
            P("wide", "narrow"),
            P("wide", "narrow"),
            P("wide", "narrow"),
            P("wide", "narrow"),
            P("wide"),
            P("wide"),
            P("wide"),
            P("wide"),
            P("wide"),
            P("wide"),
        ),
        out_specs=(
            P(None, "narrow", "wide", None),
            P(None, "narrow", "wide", None),
            P("wide", "narrow"),
            P("wide", None),
            P("wide", None),
            P("wide", "narrow"),
            P("wide", "narrow"),
            P("wide", "narrow"),
            P("wide", "narrow"),
            P("wide"),
            P("wide"),
            P("wide"),
            P("wide"),
            P("wide"),
            P("wide"),
        ),
        check_vma=False,
    )
```

```python
import functools
import math

import jax
import jax.numpy as jnp
from jax import lax
from jax.experimental import pallas as pl
from jax.experimental.pallas import tpu as pltpu
from jax.sharding import PartitionSpec as P

EPS = 1e-06
SCALE = 0.0625
LOGBASE = math.log(1000000.0)
GELU_C = 0.7978845608028654
GELU_A = 0.044715
F32, BF16 = jnp.float32, jnp.bfloat16
VMEM_LIMIT = 60 * 1024 * 1024
CHUNKS = 1
RING = 4


def call(kernel, outs, scratch=(), anys=(), smem=(), count=0, flops=0, moved=0):
    limit = (16 if moved <= 4 * 10**6 and moved != 10**6 else 60) * 1024 * 1024
    def place(index):
        if index in anys:
            return pl.BlockSpec(memory_space=pl.ANY)
        if index in smem:
            return pl.BlockSpec(memory_space=pltpu.SMEM)
        return pl.BlockSpec(memory_space=pltpu.VMEM)

    return pl.pallas_call(
        kernel,
        out_shape=[jax.ShapeDtypeStruct(s, d) for s, d in outs],
        in_specs=[place(i) for i in range(count)],
        out_specs=[pl.BlockSpec(memory_space=pltpu.VMEM)] * len(outs),
        scratch_shapes=list(scratch),
        compiler_params=pltpu.CompilerParams(vmem_limit_bytes=limit),
        cost_estimate=pl.CostEstimate(flops=1, bytes_accessed=1, transcendentals=0),
    )


def mm(a, b):
    return lax.dot_general(a, b, (((1,), (0,)), ((), ())), preferred_element_type=F32)


def mm_nt(a, b):
    return lax.dot_general(a, b, (((1,), (1,)), ((), ())), preferred_element_type=F32)


def mm_tn(a, b):
    return lax.dot_general(a, b, (((0,), (0,)), ((), ())), preferred_element_type=F32)


def root(v):
    return lax.rsqrt(jnp.mean(v * v, axis=-1, keepdims=True) + EPS)


def norm(v, gain):
    return v * root(v) * (1.0 + gain)


def norm_back(v, grad, gain):
    r = root(v)
    e = grad * (1.0 + gain)
    return r * e - v * (r * r * r * jnp.mean(e * v, axis=-1, keepdims=True))


def norm_term(v, grad):
    return jnp.sum(grad * v * root(v), axis=0, keepdims=True)


def rotate(v, cosine, sine):
    half = v.shape[-1] // 2
    a, b = v[:, :half], v[:, half:]
    return jnp.concatenate([a * cosine - b * sine, b * cosine + a * sine], axis=-1)


def rotate_back(v, cosine, sine):
    half = v.shape[-1] // 2
    a, b = v[:, :half], v[:, half:]
    return jnp.concatenate([a * cosine + b * sine, b * cosine - a * sine], axis=-1)


def tiles(extent, size):
    return [(i, min(size, extent - i)) for i in range(0, extent, size)]


def packing(q_ref, k_ref, v_ref, o_ref, g0_ref, g1_ref, g2_ref, g3_ref, g4_ref, g5_ref, out_ref):
    rows, head = q_ref.shape
    for i, ref in enumerate((q_ref, k_ref, v_ref, o_ref)):
        out_ref[:, i * head : (i + 1) * head] = ref[...]
    lane = lax.broadcasted_iota(jnp.int32, (rows, 128), 1)
    columns = jnp.zeros((rows, 128), F32)
    for i, ref in enumerate((g0_ref, g1_ref, g2_ref, g3_ref, g4_ref, g5_ref)):
        n = ref.shape[0]
        same = lax.broadcasted_iota(jnp.int32, (rows, n), 0) == lax.broadcasted_iota(
            jnp.int32, (rows, n), 1
        )
        column = jnp.sum(jnp.where(same, ref[...].astype(F32)[None, :], 0.0), axis=1, keepdims=True)
        columns = jnp.where(lane == i, column, columns)
    out_ref[:, 4 * head :] = columns.astype(BF16)


def one_hot(order, rows):
    index = lax.broadcasted_iota(jnp.int32, (rows, order.shape[1]), 0)
    return jnp.where(index == order, 1.0, 0.0).astype(BF16)


def steps(value, size, count):
    return sum(jnp.where(value >= size * i, 1, 0) for i in range(1, count))


def orders(core, width, head, wide):
    half, dw, dh = width // 2, width // wide, head // wide
    place = lax.broadcasted_iota(jnp.int32, (1, width), 1)
    side = jnp.where(place >= half, 1, 0)
    inner = place - half * side
    chip = steps(inner, dw, wide // 2)
    order = (2 * chip + ((core + side) & 1)) * dw + (inner - chip * dw)
    entry = lax.broadcasted_iota(jnp.int32, (1, head), 1)
    owner = steps(entry, dh, wide)
    chip = steps(owner, 2, wide // 2)
    pick = (((owner & 1) + core) & 1) * half + chip * dw + (entry - owner * dh)
    return order, pick


def segments(position, first, ends):
    segment = jnp.where(position < first, 0, jnp.where(position < ends, 1, 2))
    begin = jnp.where(position < first, 0, jnp.where(position < ends, first, ends))
    return segment, position - begin


def attention_forward(wide, *refs):
    x_refs, weight_refs, info_ref, refs = refs[:RING], refs[RING:-26], refs[-26], refs[-25:]
    (
        xp_ref, xn1_ref, qraw_ref, kraw_ref, q_ref, k_ref, v_ref, probs_ref, att_ref, gains_ref,
        hgain_ref, wkv_ref, wout_ref, cos_ref, sin_ref, order_ref, pick_ref, *part_refs,
        part_ref, x_ref, w_ref, sem,
    ) = refs
    head = q_ref.shape[1]
    rows, width = x_ref.shape
    half = width // 2
    slot, core, first, ends = info_ref[0], info_ref[1], info_ref[2], info_ref[3]
    copies, count = [], len(weight_refs) // 2
    for i, ref in enumerate(weight_refs):
        n = ref.shape[0]
        at = pl.multiple_of(info_ref[4 + i % count] * n + half * (1 - i // count), 16)
        copies.append(pltpu.make_async_copy(ref, w_ref.at[pl.ds(at, n)], sem.at[i]))
        copies[-1].start()
    collect(x_refs, slot, x_ref)
    order, pick = orders(core, width, head, wide)
    order_ref[...] = order
    pick_ref[...] = pick
    choose = one_hot(order, width)
    step = 128
    for r, n in tiles(rows, step):
        xp_ref[pl.ds(r, n), :] = mm(x_ref[pl.ds(r, n), :], choose).astype(BF16)
    frequency = jnp.exp(
        lax.broadcasted_iota(jnp.int32, (1, head // 2), 1).astype(F32) * (-2.0 / head) * LOGBASE
    )
    for r, n in tiles(rows, step):
        position = lax.broadcasted_iota(jnp.int32, (n, 1), 0) + r
        angle = segments(position, first, ends)[1].astype(F32) * frequency
        cos_ref[pl.ds(r, n), :] = jnp.cos(angle)
        sin_ref[pl.ds(r, n), :] = jnp.sin(angle)
    for c in copies:
        c.wait()
    columns = w_ref[:, 4 * head :].T
    gains_ref[...] = columns[:8].astype(F32)
    hgain_ref[...] = mm(columns[:8], one_hot(pick, width))
    wkv_ref[...] = w_ref[:, head : 3 * head]
    wout_ref[...] = w_ref[:, 3 * head : 4 * head]
    for r, n in tiles(rows, step):
        x = xp_ref[pl.ds(r, n), :].astype(F32)
        xn1_ref[pl.ds(r, n), :] = norm(x, gains_ref[0:1, :]).astype(BF16)
    gq, gk = hgain_ref[4:5, :], hgain_ref[5:6, :]
    raw = mm(xn1_ref[...], w_ref[:, : 3 * head])
    qraw_ref[...] = raw[:, :head]
    kraw_ref[...] = raw[:, head : 2 * head]
    v_ref[...] = raw[:, 2 * head :].astype(BF16)
    cosine, sine = cos_ref[...], sin_ref[...]
    q_ref[...] = rotate(norm(raw[:, :head], gq), cosine, sine).astype(BF16)
    k_ref[...] = rotate(norm(raw[:, head : 2 * head], gk), cosine, sine).astype(BF16)
    for r, n in tiles(rows, step):
        s = mm_nt(q_ref[pl.ds(r, n), :], k_ref[...]) * SCALE
        row = lax.broadcasted_iota(jnp.int32, s.shape, 0) + r
        col = lax.broadcasted_iota(jnp.int32, s.shape, 1)
        keep = (segments(row, first, ends)[0] == segments(col, first, ends)[0]) & (col <= row)
        s = jnp.where(keep, s, -1e30)
        e = jnp.exp(s - jnp.max(s, axis=-1, keepdims=True))
        p = e / jnp.sum(e, axis=-1, keepdims=True)
        probs_ref[pl.ds(r, n), :] = p
        att_ref[pl.ds(r, n), :] = mm(p.astype(BF16), v_ref[...]).astype(BF16)
    for r, n in tiles(rows, step):
        part_ref[pl.ds(r, n), :] = mm_nt(
            att_ref[pl.ds(r, n), :], w_ref[:, 3 * head : 4 * head]
        ).astype(BF16)
    hand_out(part_ref, slot, part_refs)


def hand_out(whole_ref, slot, refs):
    for s, ref in enumerate(refs):
        n = ref.shape[0]
        at = lax.rem(slot + s, len(refs)) * n
        ref[...] = whole_ref[pl.ds(pl.multiple_of(at, n), n), :]


def spread(whole_ref, refs):
    for s, ref in enumerate(refs):
        n = ref.shape[0]
        ref[...] = whole_ref[pl.ds((len(refs) - s) % len(refs) * n, n), :]


def collect(refs, slot, target):
    for s, ref in enumerate(refs):
        n = ref.shape[0]
        at = pl.multiple_of(lax.rem(slot + len(refs) - s, len(refs)) * n, n)
        target[pl.ds(at, n), :] = ref[...]


def total(refs):
    out = refs[0][...].astype(F32)
    for ref in refs[1:]:
        out = out + ref[...].astype(F32)
    return out


def middle_forward(*refs):
    *z_refs, xp_ref, gains_ref, slot_ref, mixed_ref, h_ref = refs[:-CHUNKS]
    n = h_ref.shape[0]
    x = xp_ref[pl.ds(pl.multiple_of(slot_ref[0] * n, n), n), :].astype(F32)
    z = total(z_refs)
    h = x + norm(z, gains_ref[1:2, :])
    mixed_ref[...] = z
    h_ref[...] = h
    xn2 = norm(h, gains_ref[2:3, :]).astype(BF16)
    for c, ref in enumerate(refs[-CHUNKS:]):
        ref[...] = xn2[c * ref.shape[0] : (c + 1) * ref.shape[0]]


def load_weights(sources, target, sem, order):
    half = sources[0].shape[1]
    waits = []
    for i in order:
        pair = [
            pltpu.make_async_copy(
                ref.at[i], target.at[i, pl.ds(j * half, half)], sem.at[2 * i + j]
            )
            for j, ref in enumerate(sources)
        ]
        for c in pair:
            c.start()
        waits.append(lambda pair=pair: [c.wait() for c in pair])
    return waits


def ffn_forward(*refs):
    wm_ref, wo_ref = refs[RING : RING + 2]
    x_ref, act_ref, fa_ref, fb_ref, *part_refs = refs[RING + 2 : -3]
    part_ref, w_ref, sem = refs[-3:]
    waits = load_weights((wm_ref, wo_ref), w_ref, sem, (0, 1, 2))
    for s in range(RING):
        n = refs[s].shape[0]
        x_ref[s * n : (s + 1) * n] = refs[s][...]
    waits[0]()
    waits[1]()
    x = x_ref[...]
    for f, n in tiles(act_ref.shape[1], 256):
        gate = mm(x, w_ref[0, :, pl.ds(f, n)])
        up = mm(x, w_ref[1, :, pl.ds(f, n)])
        square = gate * gate
        t = jnp.tanh(GELU_C * (gate + GELU_A * (gate * square)))
        bell = 0.5 * (1.0 + t)
        g = gate * bell
        slope = bell + 0.5 * gate * (1.0 - t * t) * (GELU_C * (1.0 + 3.0 * GELU_A * square))
        act_ref[:, pl.ds(f, n)] = (g * up).astype(BF16)
        fa_ref[:, pl.ds(f, n)] = (slope * up).astype(BF16)
        fb_ref[:, pl.ds(f, n)] = g.astype(BF16)
    waits[2]()
    for d, n in tiles(part_ref.shape[1], 384):
        part_ref[:, pl.ds(d, n)] = mm_nt(act_ref[...], w_ref[2, pl.ds(d, n), :]).astype(BF16)
    spread(part_ref, part_refs)


def middle_turn(chunk, *refs):
    *m_refs, h_ref, dy_ref, order_ref, info_ref, gains_ref = refs[:-4]
    out_ref, dout_ref, dm_ref, term_ref = refs[-4:]
    n = dm_ref.shape[0]
    choose = one_hot(order_ref[...], h_ref.shape[1])
    m = total(m_refs)
    gain = gains_ref[3:4, :]
    here = pl.ds(chunk * n, n)
    out = (h_ref[here, :] + norm(m, gain)).astype(BF16)
    out_ref[...] = mm_nt(out, choose).astype(BF16)
    position = lax.broadcasted_iota(jnp.int32, (n, 1), 0) + (info_ref[0] * CHUNKS + chunk) * n
    dy = mm(dy_ref[here, :], choose) * jnp.where(position < info_ref[3], 1.0, 0.0)
    dout_ref[...] = dy
    dm_ref[...] = norm_back(m, dy, gain).astype(BF16)
    term_ref[...] = norm_term(m, dy)


def ffn_backward(*refs):
    fa_ref, fb_ref, wm_ref, wo_ref = refs[RING : RING + 4]
    slot_ref, dm_ref, dg_ref, du_ref, part_ref, w_ref, sem = refs[RING + 4 :]
    waits = load_weights((wm_ref, wo_ref), w_ref, sem, (2, 0, 1))
    for s in range(RING):
        n = refs[s].shape[0]
        dm_ref[s * n : (s + 1) * n] = refs[s][...]
    waits[0]()
    dm = dm_ref[...]
    for f, n in tiles(dg_ref.shape[1], 256):
        d = mm(dm, w_ref[2, :, pl.ds(f, n)])
        dg_ref[:, pl.ds(f, n)] = (d * fa_ref[:, pl.ds(f, n)].astype(F32)).astype(BF16)
        du_ref[:, pl.ds(f, n)] = (d * fb_ref[:, pl.ds(f, n)].astype(F32)).astype(BF16)
    waits[1]()
    waits[2]()
    for d, n in tiles(part_ref.shape[1], 384):
        part = mm_nt(dg_ref[...], w_ref[0, pl.ds(d, n), :])
        part = (part + mm_nt(du_ref[...], w_ref[1, pl.ds(d, n), :])).astype(BF16)
        for s in range(RING):
            m = refs[s].shape[0]
            at = pl.multiple_of(lax.rem(slot_ref[0] + RING - s, RING) * m, m)
            part_ref[pl.ds(at, m), pl.ds(d, n)] = part[s * m : (s + 1) * m]


def weight_grad(left_ref, right_ref, own_ref, other_ref, turned_ref):
    turned_ref[...] = left_ref[...].T
    half, n_right = own_ref.shape
    for r, n in tiles(half, 192):
        for at, out in ((r, own_ref), (half + r, other_ref)):
            grad = mm(turned_ref[pl.ds(at, n), :], right_ref[:, :n_right])
            out[pl.ds(r, n), :] = grad.astype(BF16)


def ffn_weight_grads(first, *refs):
    groups = [refs[CHUNKS * i : CHUNKS * (i + 1)] for i in range(5)]
    dm, xn2, act, dg, du = groups
    *rest, turned_ref = refs[CHUNKS * 5 :]
    half, part = turned_ref.shape[0], dm[0].shape[0]
    received = rest[:3] if len(rest) == 4 else []
    outs = [rest[3].at[i] for i in range(3)] if received else rest
    for i, (left, right) in enumerate(((xn2, dg), (xn2, du), (dm, act))):
        if i != 1:
            for c, ref in enumerate(left):
                turned = ref[:, first : first + half].T
                turned_ref[:, c * part : (c + 1) * part] = turned
        for r, n in tiles(half, 192):
            grad = sum(
                mm(turned_ref[pl.ds(r, n), c * part : (c + 1) * part], right[c][...])
                for c in range(CHUNKS)
            )
            if received:
                grad = grad + received[i][pl.ds(r, n), :].astype(F32)
            outs[i][pl.ds(r, n), :] = grad.astype(BF16)


def load_heads(sources, target, sem):
    half = sources[0].shape[1]
    copies = [
        pltpu.make_async_copy(
            ref, target.at[:, pl.ds(j * half, half), :], sem.at[j]
        )
        for j, ref in enumerate(sources)
    ]
    for c in copies:
        c.start()
    return lambda: [c.wait() for c in copies]


def middle_backward(g_ref, dout_ref, h_ref, mixed_ref, gains_ref, dh_ref, dz_ref, fterm_ref, aterm_ref):
    dxn2 = g_ref[0].astype(F32)
    h, mixed = h_ref[...], mixed_ref[...]
    dh = dout_ref[...] + norm_back(h, dxn2, gains_ref[2:3, :])
    dh_ref[...] = dh
    dz_ref[...] = norm_back(mixed, dh, gains_ref[1:2, :]).astype(BF16)
    fterm_ref[...] = norm_term(h, dxn2)
    aterm_ref[...] = norm_term(mixed, dh)


def attention_backward(*refs):
    (
        slot_ref, wout_ref, qraw_ref, q_ref, k_ref, v_ref, probs_ref, hgain_ref, cos_ref, sin_ref,
        dz_ref, part_ref, term_ref, *out_refs, datt_ref, ds_ref,
    ) = refs[RING:]
    rows, head = q_ref.shape
    collect(refs[:RING], slot_ref[0], dz_ref)
    datt_ref[...] = mm(dz_ref[...], wout_ref[...]).astype(BF16)
    term = jnp.zeros((1, head), F32)
    for r, n in tiles(rows, 128):
        p = probs_ref[pl.ds(r, n), :]
        dp = mm_nt(datt_ref[pl.ds(r, n), :], v_ref[...])
        ds = (p * (dp - jnp.sum(dp * p, axis=-1, keepdims=True))).astype(BF16)
        ds_ref[pl.ds(r, n), :] = ds
        dq = (mm(ds, k_ref[...]) * SCALE).astype(BF16).astype(F32)
        cosine, sine = cos_ref[pl.ds(r, n), :], sin_ref[pl.ds(r, n), :]
        e = rotate_back(dq, cosine, sine)
        raw = qraw_ref[pl.ds(r, n), :]
        term = term + norm_term(raw, e)
        part_ref[pl.ds(r, n), :head] = norm_back(raw, e, hgain_ref[4:5, :]).astype(BF16)
    term_ref[...] = term
    part_ref[:, head : 2 * head] = (mm_tn(ds_ref[...], q_ref[...]) * SCALE).astype(BF16)
    part_ref[:, 2 * head :] = mm_tn(probs_ref[...].astype(BF16), datt_ref[...]).astype(BF16)
    hand_out(part_ref, slot_ref[0], out_refs)


def last_rows(
    g0_ref, g1_ref, g2_ref, g3_ref, xp_ref, xn1_ref, dh_ref, kraw_ref, cos_ref, sin_ref, hgain_ref, gains_ref, order_ref,
    pick_ref, slot_ref, t1_ref, t2_ref, t3_ref, qterm_ref, qm_ref, qo_ref, om_ref, oo_ref, w_ref, hm_ref, ho_ref,
    out_ref, own_ref, other_ref,
    wq_ref, hsem,
):
    head = kraw_ref.shape[1]
    n, width = dh_ref.shape
    half = width // 2
    arrived = load_heads((hm_ref, ho_ref), wq_ref, hsem)
    here = pl.ds(pl.multiple_of(slot_ref[0] * n, n), n)
    g_refs = (g0_ref, g1_ref, g2_ref, g3_ref)
    joined = sum(ref[:, head:].astype(F32) for ref in g_refs)
    dk = joined[:, :head].astype(BF16).astype(F32)
    e = rotate_back(dk, cos_ref[here, :], sin_ref[here, :])
    raw = kraw_ref[here, :]
    kterm = norm_term(raw, e)
    dkr = norm_back(raw, e, hgain_ref[5:6, :]).astype(BF16)
    dkv = jnp.concatenate([dkr, joined[:, head:].astype(BF16)], axis=1)
    dxn1 = mm_nt(dkv, w_ref[...])
    arrived()
    for i, ref in enumerate(g_refs):
        dxn1 = dxn1 + mm_nt(ref[:, :head], wq_ref[i])
    x = xp_ref[here, :].astype(F32)
    dx = (dh_ref[...] + norm_back(x, dxn1, gains_ref[0:1, :])).astype(BF16)
    term = norm_term(x, dxn1)
    choose = one_hot(order_ref[...], width)
    out_ref[...] = mm_nt(dx, choose).astype(BF16)
    grad = mm_tn(xn1_ref[here, :], dkv)
    for i, (mine, others) in enumerate(((qm_ref, qo_ref), (om_ref, oo_ref))):
        own_ref[:, i * head : (i + 1) * head] = mine[...]
        other_ref[:, i * head : (i + 1) * head] = others[...]
    own_ref[:, 2 * head : 4 * head] = grad[:half].astype(BF16)
    other_ref[:, 2 * head : 4 * head] = grad[half:].astype(BF16)
    small = jnp.concatenate([qterm_ref[...], kterm, jnp.zeros((6, head), F32)], axis=0)
    small = mm_nt(small.astype(BF16), one_hot(pick_ref[...], width))
    terms = [term, t1_ref[...], t2_ref[...], t3_ref[...], small[0:2], jnp.zeros((122, width), F32)]
    terms = jnp.concatenate(terms, axis=0).T
    own_ref[:, 4 * head :] = terms[:half].astype(BF16)
    other_ref[:, 4 * head :] = terms[half:].astype(BF16)


def finish(*refs):
    key_ref, value_ref, *rows = refs[RING:]
    head = key_ref.shape[1]
    value = total(refs[:RING])
    key_ref[...] = value[:, :head]
    value_ref[...] = value[:, head : 2 * head]
    n = value.shape[0]
    same = lax.broadcasted_iota(jnp.int32, (n, n), 0) == lax.broadcasted_iota(jnp.int32, (n, n), 1)
    for i, ref in enumerate(rows):
        column = value[:, 2 * head + i : 2 * head + i + 1]
        row = jnp.sum(jnp.where(same, column, 0.0), axis=0)
        ref[...] = row[: ref.shape[0]]


def on_device(
    tokens,
    cotangent,
    seq_lengths,
    query_weight,
    key_weight,
    value_weight,
    outproj_weight,
    gate_weight,
    up_weight,
    down_weight,
    attn_gain,
    attnout_gain,
    ffn_gain,
    ffnout_gain,
    query_gain,
    key_gain,
):
    width = tokens.shape[3]
    wide, narrow = lax.axis_size("wide"), lax.axis_size("narrow")
    chips = wide // 2
    core = lax.axis_index("wide") % 2
    slot = lax.axis_index("narrow")
    slots = jnp.reshape(slot, (1,)).astype(jnp.int32)
    same_core = [[i for i in range(wide) if i % 2 == c] for c in range(2)]
    swap = [(i, i ^ 1) for i in range(wide)]
    upward = [(i, i + 1) for i in range(narrow - 1)]
    downward = [(i + 1, i) for i in range(narrow - 1)]
    dw = width // wide
    dh = query_gain.shape[0]
    head = key_weight.shape[1]
    units = gate_weight.shape[1]
    half = width // 2

    def gather_wide(value, axis):
        return lax.all_gather(
            value, "wide", axis=axis, tiled=True, axis_index_groups=same_core
        )

    def sibling(value):
        return lax.ppermute(value, "wide", swap)

    def pair_sum(own, other):
        return (own.astype(F32) + sibling(other).astype(F32)).astype(BF16)

    def scatter_wide(value, axis):
        return lax.psum_scatter(
            value, "wide", scatter_dimension=axis, tiled=True, axis_index_groups=same_core
        )

    def after(value, *others):
        return lax.optimization_barrier((value, *others))[0]

    def gather_rows(value):
        return lax.all_gather(value, "narrow", axis=0, tiled=True)

    def gather_ring(value):
        return pass_on([value] * narrow)

    def pass_on(parts):
        got = [parts[0]]
        for s in range(1, narrow):
            shift = [(i, (i + s) % narrow) for i in range(narrow)]
            got.append(lax.ppermute(parts[s], "narrow", shift))
        return got

    def exchange_z(value):
        parts = value.reshape(narrow, -1, value.shape[-1])
        return lax.all_to_all(parts, "narrow", split_axis=0, concat_axis=0, tiled=True)

    def enter(value):
        value = value.reshape(value.shape[0], value.shape[2], width)
        value = lax.all_to_all(value, "wide", split_axis=0, concat_axis=0, tiled=True)
        return value.reshape(-1, width)

    def leave(value):
        value = value.reshape(wide, -1, width)
        value = lax.all_to_all(value, "wide", split_axis=0, concat_axis=0, tiled=True)
        return value.reshape(wide, 1, -1, width)

    bf, ff = BF16, F32
    pack = call(packing, [((dw, 4 * head + 128), bf)], count=10, flops=10**6, moved=10**6)(
        query_weight, key_weight, value_weight, outproj_weight,
        attn_gain, attnout_gain, ffn_gain, ffnout_gain, query_gain, key_gain,
    )[0]
    wa_mine = gather_wide(pack, 0)
    lengths = seq_lengths[0]
    info = jnp.stack([slot, core, lengths[0], lengths[0] + lengths[1], 0]).astype(jnp.int32)
    queries = gather_ring(query_weight)
    own_x = after(enter(tokens), info, *queries)
    quarter = own_x.shape[0]
    rows = quarter * narrow
    part = quarter // CHUNKS
    every = range(CHUNKS)
    sem = pltpu.SemaphoreType.DMA
    f_scratch = pltpu.VMEM((3, width, units), bf)
    x_all = gather_ring(own_x)
    wf_mine = gather_wide(after(jnp.stack([gate_weight, up_weight, down_weight]), own_x), 1)
    weights = [sibling(after(wa_mine, *x_all)), wa_mine]
    wh_mine = gather_wide(after(jnp.stack(queries), wf_mine), 1)
    own_dy = enter(after(cotangent, own_x))
    many = len(x_all) + len(weights)
    (
        xp, xn1, qraw, kraw, q, k, v, probs, attended, gains, hgain, wkv, wout, cosine, sine, order, pick,
        *z_parts,
    ) = call(
        functools.partial(attention_forward, wide),
        [
            ((rows, width), bf), ((rows, width), bf), ((rows, head), ff), ((rows, head), ff),
            ((rows, head), bf), ((rows, head), bf), ((rows, head), bf), ((rows, rows), ff),
            ((rows, head), bf), ((8, width), ff), ((8, head), ff), ((width, 2 * head), bf), ((width, head), bf),
            ((rows, head // 2), ff), ((rows, head // 2), ff), ((1, width), jnp.int32),
            ((1, head), jnp.int32),
        ]
        + [((quarter, width), bf)] * narrow,
        scratch=[
            pltpu.VMEM((rows, width), bf), pltpu.VMEM((rows, width), bf),
            pltpu.VMEM((width, 4 * head + 128), bf), sem((len(weights),)),
        ],
        anys=tuple(range(len(x_all), many)), smem=(many,), count=many + 1,
        flops=3 * 10**9, moved=8 * 10**6,
    )(*x_all, *weights, info)
    z = pass_on(z_parts)
    mixed, h, *xn2_own = call(
        middle_forward,
        [((quarter, width), ff)] * 2 + [((part, width), bf)] * CHUNKS,
        smem=(narrow + 2,), count=narrow + 3, flops=10**7, moved=2 * 10**6,
    )(*z, xp, gains, slots)
    xn2 = [gather_ring(xn2_own[c]) for c in every]
    wf_other = sibling(after(wf_mine, xn2[0][1], xn2[0][-1]))
    def ffn_ahead(c):
        return call(
            ffn_forward,
            [((narrow * part, width), bf)] + [((narrow * part, units), bf)] * 3
            + [((part, width), bf)] * narrow,
            scratch=[pltpu.VMEM((narrow * part, width), bf), f_scratch, sem((6,))],
            anys=(narrow, narrow + 1), count=narrow + 2, flops=3 * 10**9, moved=16 * 10**6,
        )(*xn2[c], wf_mine, wf_other)

    ahead = []
    for c in every:
        if c:
            xn2[c][0] = after(xn2[c][0], ahead[-1][1])
        ahead.append(ffn_ahead(c))
    xn2_all, act, fa, fb, *m_part = zip(*ahead)
    m = [pass_on([p[c] for p in m_part]) for c in every]
    out_own, d_out, dm_own, turn_term = zip(*[
        call(
            functools.partial(middle_turn, c),
            [((part, width), bf), ((part, width), ff), ((part, width), bf), ((1, width), ff)],
            smem=(narrow + 3,), count=narrow + 5, flops=10**8, moved=4 * 10**6,
        )(*m[c], h, own_dy, order, info, gains)
        for c in every
    ])
    dm = [gather_ring(dm_own[c]) for c in every]

    dm[0][0] = after(dm[0][0], wh_mine)

    def ffn_back(c):
        return call(
            ffn_backward,
            [((narrow * part, width), bf)] + [((narrow * part, units), bf)] * 2
            + [((narrow * part, width), bf)],
            scratch=[f_scratch, sem((6,))],
            anys=(narrow + 2, narrow + 3), smem=(narrow + 4,), count=narrow + 5,
            flops=3 * 10**9, moved=16 * 10**6,
        )(*dm[c], fa[c], fb[c], wf_mine, wf_other, slots)

    back = []
    for c in every:
        if c:
            dm[c][0] = after(dm[c][0], back[-1][1])
        back.append(ffn_back(c))
    dm_all, d_gate, d_up, dxn2_part = zip(*back)
    dxn2 = lax.psum_scatter(
        dxn2_part[0].reshape(narrow, quarter, width), "narrow", scatter_dimension=0, tiled=True
    )
    saved = (*dm_all, *xn2_all, *act, *d_gate, *d_up)

    def ffn_grads(first, *received):
        outs = [((3, half, units), bf)] if received else [((half, units), bf)] * 3
        return call(
            functools.partial(ffn_weight_grads, first),
            outs,
            scratch=[pltpu.VMEM((half, rows), bf)],
            count=5 * CHUNKS + len(received), flops=10**6, moved=10**6,
        )(*saved, *received)

    ffn_other = [sibling(g) for g in ffn_grads(half)]
    ffn_sum = ffn_grads(0, *ffn_other)[0]
    dxn2 = after(dxn2, ffn_sum)
    s_ffn = scatter_wide(ffn_sum, 1)
    left_out = leave(out_own[0])
    d_resid, dz_own, ffn_term, attnout_term = call(
        middle_backward,
        [((quarter, width), ff), ((quarter, width), bf), ((1, width), ff), ((1, width), ff)],
        count=5, flops=10**7, moved=3 * 10**6,
    )(dxn2, d_out[0], h, mixed, gains)
    dz = gather_ring(dz_own)
    wh_other = sibling(after(wh_mine, dz_own))
    dz_all, joined_part, query_term, *joined = call(
        attention_backward,
        [((rows, width), bf), ((rows, 3 * head), bf), ((1, head), ff)]
        + [((quarter, 3 * head), bf)] * narrow,
        scratch=[pltpu.VMEM((rows, head), bf), pltpu.VMEM((rows, rows), bf)],
        smem=(narrow,), count=narrow + 10, flops=2 * 10**9, moved=6 * 10**6,
    )(*dz, slots, wout, qraw, q, k, v, probs, hgain, cosine, sine)
    joined = pass_on(joined)

    def outer(left, right, columns):
        return call(
            weight_grad,
            [((half, columns), bf)] * 2,
            scratch=[pltpu.VMEM((width, left.shape[0]), bf)],
            count=2, flops=2 * width * left.shape[0] * columns, moved=3 * 10**6,
        )(left, right)

    g_query = outer(xn1, joined_part, head)
    g_outproj = outer(dz_all, attended, head)
    joined[0] = after(joined[0], left_out, *g_query, *g_outproj)
    heads = wh_mine.shape[0]
    dx_own, own, other = call(
        last_rows,
        [((quarter, width), bf)] + [((half, 4 * head + 128), bf)] * 2,
        scratch=[pltpu.VMEM((heads, width, head), bf), sem((2,))],
        smem=(14,), anys=(24, 25), count=26, flops=10**9, moved=8 * 10**6,
    )(
        *joined, xp, xn1, d_resid, kraw, cosine, sine, hgain, gains, order, pick, slots,
        attnout_term, ffn_term, *turn_term, query_term, *g_query, *g_outproj, wkv,
        wh_mine, wh_other,
    )

    def scatter_chips(value):
        parts = value.reshape(chips, dw, value.shape[1])
        parts = lax.all_to_all(
            parts, "wide", split_axis=0, concat_axis=0, tiled=True, axis_index_groups=same_core
        )
        return parts.astype(F32).sum(axis=0)

    last = scatter_chips(pair_sum(own, other))
    s_query, s_outproj = last[:, :head], last[:, head : 2 * head]
    last = last[:, 2 * head :].astype(BF16)
    last, s_ffn, dx_own = lax.optimization_barrier((last, s_ffn, dx_own))
    s_ffn = s_ffn.astype(F32)
    left_dx, shared = leave(dx_own), gather_ring(last)
    left_dx, *shared = lax.optimization_barrier((left_dx, *shared))
    small = call(
        finish,
        [((dw, head), ff)] * 2 + [((dw,), ff)] * 4 + [((dh,), ff)] * 2,
        count=narrow, flops=10**6, moved=2 * 10**6,
    )(*shared)
    return (left_out, left_dx, s_query, *small[:2], s_outproj, s_ffn[0], s_ffn[1], s_ffn[2], *small[2:])


def solution(mesh):
    return jax.shard_map(
        on_device,
        mesh=mesh,
        in_specs=(
            P(None, "narrow", "wide", None),
            P(None, "narrow", "wide", None),
            P("wide", None),
            P("wide", "narrow"),
            P("wide", None),
            P("wide", None),
            P("wide", "narrow"),
            P("wide", "narrow"),
            P("wide", "narrow"),
            P("wide", "narrow"),
            P("wide"),
            P("wide"),
            P("wide"),
            P("wide"),
            P("wide"),
            P("wide"),
        ),
        out_specs=(
            P(None, "narrow", "wide", None),
            P(None, "narrow", "wide", None),
            P("wide", "narrow"),
            P("wide", None),
            P("wide", None),
            P("wide", "narrow"),
            P("wide", "narrow"),
            P("wide", "narrow"),
            P("wide", "narrow"),
            P("wide"),
            P("wide"),
            P("wide"),
            P("wide"),
            P("wide"),
            P("wide"),
        ),
        check_vma=False,
    )
```

```python
import functools
import math

import jax
import jax.numpy as jnp
from jax import lax
from jax.experimental import pallas as pl
from jax.experimental.pallas import tpu as pltpu
from jax.sharding import PartitionSpec as P

EPS = 1e-06
SCALE = 0.0625
LOGBASE = math.log(1000000.0)
GELU_C = 0.7978845608028654
GELU_A = 0.044715
F32, BF16 = jnp.float32, jnp.bfloat16
VMEM_LIMIT = 60 * 1024 * 1024
CHUNKS = 1
RING = 4
FFN_TILE = 512


def call(kernel, outs, scratch=(), anys=(), smem=(), count=0, flops=0, moved=0, far=0):
    limit = (16 if moved <= 4 * 10**6 and moved != 10**6 else 60) * 1024 * 1024
    def place(index):
        if index in anys:
            return pl.BlockSpec(memory_space=pl.ANY)
        if index in smem:
            return pl.BlockSpec(memory_space=pltpu.SMEM)
        return pl.BlockSpec(memory_space=pltpu.VMEM)

    return pl.pallas_call(
        kernel,
        out_shape=[jax.ShapeDtypeStruct(s, d) for s, d in outs],
        in_specs=[place(i) for i in range(count)],
        out_specs=[
            pl.BlockSpec(memory_space=pl.ANY if i < far else pltpu.VMEM) for i in range(len(outs))
        ],
        scratch_shapes=list(scratch),
        compiler_params=pltpu.CompilerParams(vmem_limit_bytes=limit),
        cost_estimate=pl.CostEstimate(flops=1, bytes_accessed=1, transcendentals=0),
    )


def mm(a, b):
    return lax.dot_general(a, b, (((1,), (0,)), ((), ())), preferred_element_type=F32)


def mm_nt(a, b):
    return lax.dot_general(a, b, (((1,), (1,)), ((), ())), preferred_element_type=F32)


def mm_tn(a, b):
    return lax.dot_general(a, b, (((0,), (0,)), ((), ())), preferred_element_type=F32)


def root(v):
    return lax.rsqrt(jnp.mean(v * v, axis=-1, keepdims=True) + EPS)


def norm(v, gain):
    return v * root(v) * (1.0 + gain)


def norm_back(v, grad, gain):
    r = root(v)
    e = grad * (1.0 + gain)
    return r * e - v * (r * r * r * jnp.mean(e * v, axis=-1, keepdims=True))


def norm_term(v, grad):
    return jnp.sum(grad * v * root(v), axis=0, keepdims=True)


def rotate(v, cosine, sine):
    half = v.shape[-1] // 2
    a, b = v[:, :half], v[:, half:]
    return jnp.concatenate([a * cosine - b * sine, b * cosine + a * sine], axis=-1)


def rotate_back(v, cosine, sine):
    half = v.shape[-1] // 2
    a, b = v[:, :half], v[:, half:]
    return jnp.concatenate([a * cosine + b * sine, b * cosine - a * sine], axis=-1)


def tiles(extent, size):
    return [(i, min(size, extent - i)) for i in range(0, extent, size)]


def packing(q_ref, k_ref, v_ref, o_ref, g0_ref, g1_ref, g2_ref, g3_ref, g4_ref, g5_ref, out_ref):
    rows, head = q_ref.shape
    for i, ref in enumerate((q_ref, k_ref, v_ref, o_ref)):
        out_ref[:, i * head : (i + 1) * head] = ref[...]
    lane = lax.broadcasted_iota(jnp.int32, (rows, 128), 1)
    columns = jnp.zeros((rows, 128), F32)
    for i, ref in enumerate((g0_ref, g1_ref, g2_ref, g3_ref, g4_ref, g5_ref)):
        n = ref.shape[0]
        same = lax.broadcasted_iota(jnp.int32, (rows, n), 0) == lax.broadcasted_iota(
            jnp.int32, (rows, n), 1
        )
        column = jnp.sum(jnp.where(same, ref[...].astype(F32)[None, :], 0.0), axis=1, keepdims=True)
        columns = jnp.where(lane == i, column, columns)
    out_ref[:, 4 * head :] = columns.astype(BF16)


def one_hot(order, rows):
    index = lax.broadcasted_iota(jnp.int32, (rows, order.shape[1]), 0)
    return jnp.where(index == order, 1.0, 0.0).astype(BF16)


def steps(value, size, count):
    return sum(jnp.where(value >= size * i, 1, 0) for i in range(1, count))


def orders(core, width, head, wide):
    half, dw, dh = width // 2, width // wide, head // wide
    place = lax.broadcasted_iota(jnp.int32, (1, width), 1)
    side = jnp.where(place >= half, 1, 0)
    inner = place - half * side
    chip = steps(inner, dw, wide // 2)
    order = (2 * chip + ((core + side) & 1)) * dw + (inner - chip * dw)
    entry = lax.broadcasted_iota(jnp.int32, (1, head), 1)
    owner = steps(entry, dh, wide)
    chip = steps(owner, 2, wide // 2)
    pick = (((owner & 1) + core) & 1) * half + chip * dw + (entry - owner * dh)
    return order, pick


def segments(position, first, ends):
    segment = jnp.where(position < first, 0, jnp.where(position < ends, 1, 2))
    begin = jnp.where(position < first, 0, jnp.where(position < ends, first, ends))
    return segment, position - begin


def rope_tables(info_ref, cos_ref, sin_ref):
    rows, half = cos_ref.shape
    frequency = jnp.exp(
        lax.broadcasted_iota(jnp.int32, (1, half), 1).astype(F32) * (-1.0 / half) * LOGBASE
    )
    for r, n in tiles(rows, 128):
        position = lax.broadcasted_iota(jnp.int32, (n, 1), 0) + r
        angle = segments(position, info_ref[2], info_ref[3])[1].astype(F32) * frequency
        cos_ref[pl.ds(r, n), :] = jnp.cos(angle)
        sin_ref[pl.ds(r, n), :] = jnp.sin(angle)


def attention_forward(wide, *refs):
    x_refs, weight_refs, refs = refs[:RING], refs[RING:-32], refs[-32:]
    info_ref, cos_ref, sin_ref, *refs = refs
    (
        *far_refs, wkv_ref, wout_ref, q_ref, k_ref, v_ref, att_ref, gains_ref,
        hgain_ref, order_ref, pick_ref,
    ) = refs[:15]
    part_refs, near_refs = refs[15:-10], refs[-10:-5]
    xp_ref, xn1_ref, qraw_ref, kraw_ref, probs_ref = near_refs
    part_ref, x_ref, w_ref, sem, out_sem = refs[-5:]
    leaving = []

    def leave(here, there):
        leaving.append(pltpu.make_async_copy(here, there, out_sem.at[len(leaving)]))
        leaving[-1].start()

    head = q_ref.shape[1]
    rows, width = x_ref.shape
    half = width // 2
    slot, core, first, ends = info_ref[0], info_ref[1], info_ref[2], info_ref[3]
    copies, count = [], len(weight_refs) // 2
    for i, ref in enumerate(weight_refs):
        n = ref.shape[0]
        at = pl.multiple_of(info_ref[4 + i % count] * n + half * (1 - i // count), 16)
        copies.append(pltpu.make_async_copy(ref, w_ref.at[pl.ds(at, n)], sem.at[i]))
        copies[-1].start()
    collect(x_refs, slot, x_ref)
    order, pick = orders(core, width, head, wide)
    order_ref[...] = order
    pick_ref[...] = pick
    choose = one_hot(order, width)
    step = 128
    for r, n in tiles(rows, step):
        xp_ref[pl.ds(r, n), :] = mm(x_ref[pl.ds(r, n), :], choose).astype(BF16)
    leave(xp_ref, far_refs[0])
    for c in copies:
        c.wait()
    columns = w_ref[:, 4 * head :].T
    gains_ref[...] = columns[:8].astype(F32)
    hgain_ref[...] = mm(columns[:8], one_hot(pick, width))
    leave(w_ref.at[:, pl.ds(head, 2 * head)], wkv_ref)
    leave(w_ref.at[:, pl.ds(3 * head, head)], wout_ref)
    for r, n in tiles(rows, step):
        x = xp_ref[pl.ds(r, n), :].astype(F32)
        xn1_ref[pl.ds(r, n), :] = norm(x, gains_ref[0:1, :]).astype(BF16)
    leave(xn1_ref, far_refs[1])
    gq, gk = hgain_ref[4:5, :], hgain_ref[5:6, :]
    raw = mm(xn1_ref[...], w_ref[:, : 3 * head])
    qraw_ref[...] = raw[:, :head]
    kraw_ref[...] = raw[:, head : 2 * head]
    leave(qraw_ref, far_refs[2])
    leave(kraw_ref, far_refs[3])
    v_ref[...] = raw[:, 2 * head :].astype(BF16)
    cosine, sine = cos_ref[...], sin_ref[...]
    q_ref[...] = rotate(norm(raw[:, :head], gq), cosine, sine).astype(BF16)
    k_ref[...] = rotate(norm(raw[:, head : 2 * head], gk), cosine, sine).astype(BF16)
    for r, n in tiles(rows, step):
        s = mm_nt(q_ref[pl.ds(r, n), :], k_ref[...]) * SCALE
        row = lax.broadcasted_iota(jnp.int32, s.shape, 0) + r
        col = lax.broadcasted_iota(jnp.int32, s.shape, 1)
        keep = (segments(row, first, ends)[0] == segments(col, first, ends)[0]) & (col <= row)
        s = jnp.where(keep, s, -1e30)
        e = jnp.exp(s - jnp.max(s, axis=-1, keepdims=True))
        p = e / jnp.sum(e, axis=-1, keepdims=True)
        probs_ref[pl.ds(r, n), :] = p
        att_ref[pl.ds(r, n), :] = mm(p.astype(BF16), v_ref[...]).astype(BF16)
    leave(probs_ref, far_refs[4])
    for r, n in tiles(rows, step):
        part_ref[pl.ds(r, n), :] = mm_nt(
            att_ref[pl.ds(r, n), :], w_ref[:, 3 * head : 4 * head]
        ).astype(BF16)
    hand_out(part_ref, slot, part_refs)
    for c in leaving:
        c.wait()


def hand_out(whole_ref, slot, refs):
    for s, ref in enumerate(refs):
        n = ref.shape[0]
        at = lax.rem(slot + s, len(refs)) * n
        ref[...] = whole_ref[pl.ds(pl.multiple_of(at, n), n), :]


def spread(whole_ref, refs):
    for s, ref in enumerate(refs):
        n = ref.shape[0]
        ref[...] = whole_ref[pl.ds((len(refs) - s) % len(refs) * n, n), :]


def collect(refs, slot, target):
    for s, ref in enumerate(refs):
        n = ref.shape[0]
        at = pl.multiple_of(lax.rem(slot + len(refs) - s, len(refs)) * n, n)
        target[pl.ds(at, n), :] = ref[...]


def total(refs):
    out = refs[0][...].astype(F32)
    for ref in refs[1:]:
        out = out + ref[...].astype(F32)
    return out


def middle_forward(*refs):
    *z_refs, xp_ref, gains_ref, slot_ref, mixed_ref, h_ref = refs[:-CHUNKS]
    n = h_ref.shape[0]
    x = xp_ref[pl.ds(pl.multiple_of(slot_ref[0] * n, n), n), :].astype(F32)
    z = total(z_refs)
    h = x + norm(z, gains_ref[1:2, :])
    mixed_ref[...] = z
    h_ref[...] = h
    xn2 = norm(h, gains_ref[2:3, :]).astype(BF16)
    for c, ref in enumerate(refs[-CHUNKS:]):
        ref[...] = xn2[c * ref.shape[0] : (c + 1) * ref.shape[0]]


def load_weights(sources, target, sem, order):
    half = sources[0].shape[1]
    waits = []
    for i in order:
        pair = [
            pltpu.make_async_copy(
                ref.at[i], target.at[i, pl.ds(j * half, half)], sem.at[2 * i + j]
            )
            for j, ref in enumerate(sources)
        ]
        for c in pair:
            c.start()
        waits.append(lambda pair=pair: [c.wait() for c in pair])
    return waits


def ffn_forward(*refs):
    wm_ref, wo_ref = refs[RING : RING + 2]
    x_out, act_out, fa_out, fb_out, *part_refs = refs[RING + 2 : -9]
    x_ref, act_ref, fa_ref, fb_ref, part_ref, w_ref, sem, down_sem, out_sem = refs[-9:]
    half = wm_ref.shape[1]
    cuts = tiles(act_ref.shape[1], FFN_TILE)
    loads = []
    for t, (f, n) in enumerate(cuts):
        columns = pl.ds(f, n)
        group = [
            pltpu.make_async_copy(
                ref.at[i, :, columns],
                w_ref.at[i, pl.ds(j * half, half), columns],
                sem.at[t, 2 * i + j],
            )
            for i in (0, 1)
            for j, ref in enumerate((wm_ref, wo_ref))
        ]
        for c in group:
            c.start()
        loads.append(group)
    down = [
        pltpu.make_async_copy(ref.at[2], w_ref.at[2, pl.ds(j * half, half)], down_sem.at[j])
        for j, ref in enumerate((wm_ref, wo_ref))
    ]
    for c in down:
        c.start()
    for s in range(RING):
        n = refs[s].shape[0]
        x_ref[s * n : (s + 1) * n] = refs[s][...]
    leaving = [pltpu.make_async_copy(x_ref, x_out, out_sem.at[0, 0])]
    leaving[0].start()
    x = x_ref[...]
    for t, (f, n) in enumerate(cuts):
        columns = pl.ds(f, n)
        for c in loads[t]:
            c.wait()
        gate = mm(x, w_ref[0, :, columns])
        up = mm(x, w_ref[1, :, columns])
        square = gate * gate
        th = jnp.tanh(GELU_C * (gate + GELU_A * (gate * square)))
        bell = 0.5 * (1.0 + th)
        g = gate * bell
        slope = bell + 0.5 * gate * (1.0 - th * th) * (GELU_C * (1.0 + 3.0 * GELU_A * square))
        act_ref[:, columns] = (g * up).astype(BF16)
        fa_ref[:, columns] = (slope * up).astype(BF16)
        fb_ref[:, columns] = g.astype(BF16)
        pairs = ((act_ref, act_out), (fa_ref, fa_out), (fb_ref, fb_out))
        for i, (here, there) in enumerate(pairs):
            c = pltpu.make_async_copy(
                here.at[:, columns], there.at[:, columns], out_sem.at[1 + t, i]
            )
            c.start()
            leaving.append(c)
    for c in down:
        c.wait()
    for d, n in tiles(part_ref.shape[1], 384):
        part_ref[:, pl.ds(d, n)] = mm_nt(act_ref[...], w_ref[2, pl.ds(d, n), :]).astype(BF16)
    spread(part_ref, part_refs)
    for c in leaving:
        c.wait()


def middle_turn(chunk, *refs):
    *m_refs, h_ref, dy_ref, order_ref, info_ref, gains_ref = refs[:-4]
    out_ref, dout_ref, dm_ref, term_ref = refs[-4:]
    n = dm_ref.shape[0]
    choose = one_hot(order_ref[...], h_ref.shape[1])
    m = total(m_refs)
    gain = gains_ref[3:4, :]
    here = pl.ds(chunk * n, n)
    out = (h_ref[here, :] + norm(m, gain)).astype(BF16)
    out_ref[...] = mm_nt(out, choose).astype(BF16)
    position = lax.broadcasted_iota(jnp.int32, (n, 1), 0) + (info_ref[0] * CHUNKS + chunk) * n
    dy = mm(dy_ref[here, :], choose) * jnp.where(position < info_ref[3], 1.0, 0.0)
    dout_ref[...] = dy
    dm_ref[...] = norm_back(m, dy, gain).astype(BF16)
    term_ref[...] = norm_term(m, dy)


def ffn_backward(*refs):
    fa_ref, fb_ref, wm_ref, wo_ref = refs[RING : RING + 4]
    slot_ref, dm_ref, dg_ref, du_ref, part_ref, w_ref, sem = refs[RING + 4 :]
    waits = load_weights((wm_ref, wo_ref), w_ref, sem, (2, 0, 1))
    for s in range(RING):
        n = refs[s].shape[0]
        dm_ref[s * n : (s + 1) * n] = refs[s][...]
    waits[0]()
    dm = dm_ref[...]
    for f, n in tiles(dg_ref.shape[1], 256):
        d = mm(dm, w_ref[2, :, pl.ds(f, n)])
        dg_ref[:, pl.ds(f, n)] = (d * fa_ref[:, pl.ds(f, n)].astype(F32)).astype(BF16)
        du_ref[:, pl.ds(f, n)] = (d * fb_ref[:, pl.ds(f, n)].astype(F32)).astype(BF16)
    waits[1]()
    waits[2]()
    for d, n in tiles(part_ref.shape[1], 384):
        part = mm_nt(dg_ref[...], w_ref[0, pl.ds(d, n), :])
        part = (part + mm_nt(du_ref[...], w_ref[1, pl.ds(d, n), :])).astype(BF16)
        for s in range(RING):
            m = refs[s].shape[0]
            at = pl.multiple_of(lax.rem(slot_ref[0] + RING - s, RING) * m, m)
            part_ref[pl.ds(at, m), pl.ds(d, n)] = part[s * m : (s + 1) * m]


def weight_grad(left_ref, right_ref, own_ref, other_ref, turned_ref):
    turned_ref[...] = left_ref[...].T
    half, n_right = own_ref.shape
    for r, n in tiles(half, 192):
        for at, out in ((r, own_ref), (half + r, other_ref)):
            grad = mm(turned_ref[pl.ds(at, n), :], right_ref[:, :n_right])
            out[pl.ds(r, n), :] = grad.astype(BF16)


def ffn_weight_grads(first, *refs):
    groups = [refs[CHUNKS * i : CHUNKS * (i + 1)] for i in range(5)]
    dm, xn2, act, dg, du = groups
    *rest, turned_ref = refs[CHUNKS * 5 :]
    half, part = turned_ref.shape[0], dm[0].shape[0]
    received = rest[:3] if len(rest) == 4 else []
    outs = [rest[3].at[i] for i in range(3)] if received else rest
    for i, (left, right) in enumerate(((xn2, dg), (xn2, du), (dm, act))):
        if i != 1:
            for c, ref in enumerate(left):
                turned = ref[:, first : first + half].T
                turned_ref[:, c * part : (c + 1) * part] = turned
        for r, n in tiles(half, 192):
            grad = sum(
                mm(turned_ref[pl.ds(r, n), c * part : (c + 1) * part], right[c][...])
                for c in range(CHUNKS)
            )
            if received:
                grad = grad + received[i][pl.ds(r, n), :].astype(F32)
            outs[i][pl.ds(r, n), :] = grad.astype(BF16)


def load_heads(sources, target, sem):
    half = sources[0].shape[1]
    copies = [
        pltpu.make_async_copy(
            ref, target.at[:, pl.ds(j * half, half), :], sem.at[j]
        )
        for j, ref in enumerate(sources)
    ]
    for c in copies:
        c.start()
    return lambda: [c.wait() for c in copies]


def middle_backward(g_ref, dout_ref, h_ref, mixed_ref, gains_ref, dh_ref, dz_ref, fterm_ref, aterm_ref):
    dxn2 = g_ref[0].astype(F32)
    h, mixed = h_ref[...], mixed_ref[...]
    dh = dout_ref[...] + norm_back(h, dxn2, gains_ref[2:3, :])
    dh_ref[...] = dh
    dz_ref[...] = norm_back(mixed, dh, gains_ref[1:2, :]).astype(BF16)
    fterm_ref[...] = norm_term(h, dxn2)
    aterm_ref[...] = norm_term(mixed, dh)


def attention_backward(*refs):
    (
        slot_ref, wout_ref, qraw_ref, q_ref, k_ref, v_ref, probs_ref, hgain_ref, cos_ref, sin_ref,
        dz_ref, part_ref, term_ref, *out_refs, datt_ref, ds_ref,
    ) = refs[RING:]
    rows, head = q_ref.shape
    collect(refs[:RING], slot_ref[0], dz_ref)
    datt_ref[...] = mm(dz_ref[...], wout_ref[...]).astype(BF16)
    term = jnp.zeros((1, head), F32)
    for r, n in tiles(rows, 128):
        p = probs_ref[pl.ds(r, n), :]
        dp = mm_nt(datt_ref[pl.ds(r, n), :], v_ref[...])
        ds = (p * (dp - jnp.sum(dp * p, axis=-1, keepdims=True))).astype(BF16)
        ds_ref[pl.ds(r, n), :] = ds
        dq = (mm(ds, k_ref[...]) * SCALE).astype(BF16).astype(F32)
        cosine, sine = cos_ref[pl.ds(r, n), :], sin_ref[pl.ds(r, n), :]
        e = rotate_back(dq, cosine, sine)
        raw = qraw_ref[pl.ds(r, n), :]
        term = term + norm_term(raw, e)
        part_ref[pl.ds(r, n), :head] = norm_back(raw, e, hgain_ref[4:5, :]).astype(BF16)
    term_ref[...] = term
    part_ref[:, head : 2 * head] = (mm_tn(ds_ref[...], q_ref[...]) * SCALE).astype(BF16)
    part_ref[:, 2 * head :] = mm_tn(probs_ref[...].astype(BF16), datt_ref[...]).astype(BF16)
    hand_out(part_ref, slot_ref[0], out_refs)


def last_rows(
    g0_ref, g1_ref, g2_ref, g3_ref, xp_ref, xn1_ref, dh_ref, kraw_ref, cos_ref, sin_ref, hgain_ref, gains_ref, order_ref,
    pick_ref, slot_ref, t1_ref, t2_ref, t3_ref, qterm_ref, qm_ref, qo_ref, om_ref, oo_ref, w_ref, hm_ref, ho_ref,
    out_ref, own_ref, other_ref,
    wq_ref, hsem, x_here, xn1_here, raw_here, cos_here, sin_here, row_sem,
):
    head = kraw_ref.shape[1]
    n, width = dh_ref.shape
    half = width // 2
    arrived = load_heads((hm_ref, ho_ref), wq_ref, hsem)
    here = pl.ds(pl.multiple_of(slot_ref[0] * n, n), n)
    rows = [
        pltpu.make_async_copy(ref.at[here], target, row_sem.at[i])
        for i, (ref, target) in enumerate((
            (kraw_ref, raw_here), (cos_ref, cos_here), (sin_ref, sin_here), (xn1_ref, xn1_here),
            (xp_ref, x_here),
        ))
    ]
    for c in rows:
        c.start()
    g_refs = (g0_ref, g1_ref, g2_ref, g3_ref)
    joined = sum(ref[:, head:].astype(F32) for ref in g_refs)
    dk = joined[:, :head].astype(BF16).astype(F32)
    for c in rows:
        c.wait()
    e = rotate_back(dk, cos_here[...], sin_here[...])
    raw = raw_here[...]
    kterm = norm_term(raw, e)
    dkr = norm_back(raw, e, hgain_ref[5:6, :]).astype(BF16)
    dkv = jnp.concatenate([dkr, joined[:, head:].astype(BF16)], axis=1)
    dxn1 = mm_nt(dkv, w_ref[...])
    arrived()
    for i, ref in enumerate(g_refs):
        dxn1 = dxn1 + mm_nt(ref[:, :head], wq_ref[i])
    x = x_here[...].astype(F32)
    dx = (dh_ref[...] + norm_back(x, dxn1, gains_ref[0:1, :])).astype(BF16)
    term = norm_term(x, dxn1)
    choose = one_hot(order_ref[...], width)
    out_ref[...] = mm_nt(dx, choose).astype(BF16)
    grad = mm_tn(xn1_here[...], dkv)
    for i, (mine, others) in enumerate(((qm_ref, qo_ref), (om_ref, oo_ref))):
        own_ref[:, i * head : (i + 1) * head] = mine[...]
        other_ref[:, i * head : (i + 1) * head] = others[...]
    own_ref[:, 2 * head : 4 * head] = grad[:half].astype(BF16)
    other_ref[:, 2 * head : 4 * head] = grad[half:].astype(BF16)
    small = jnp.concatenate([qterm_ref[...], kterm, jnp.zeros((6, head), F32)], axis=0)
    small = mm_nt(small.astype(BF16), one_hot(pick_ref[...], width))
    terms = [term, t1_ref[...], t2_ref[...], t3_ref[...], small[0:2], jnp.zeros((122, width), F32)]
    terms = jnp.concatenate(terms, axis=0).T
    own_ref[:, 4 * head :] = terms[:half].astype(BF16)
    other_ref[:, 4 * head :] = terms[half:].astype(BF16)


def finish(*refs):
    key_ref, value_ref, *rows = refs[RING:]
    head = key_ref.shape[1]
    value = total(refs[:RING])
    key_ref[...] = value[:, :head]
    value_ref[...] = value[:, head : 2 * head]
    n = value.shape[0]
    same = lax.broadcasted_iota(jnp.int32, (n, n), 0) == lax.broadcasted_iota(jnp.int32, (n, n), 1)
    for i, ref in enumerate(rows):
        column = value[:, 2 * head + i : 2 * head + i + 1]
        row = jnp.sum(jnp.where(same, column, 0.0), axis=0)
        ref[...] = row[: ref.shape[0]]


def on_device(
    tokens,
    cotangent,
    seq_lengths,
    query_weight,
    key_weight,
    value_weight,
    outproj_weight,
    gate_weight,
    up_weight,
    down_weight,
    attn_gain,
    attnout_gain,
    ffn_gain,
    ffnout_gain,
    query_gain,
    key_gain,
):
    width = tokens.shape[3]
    wide, narrow = lax.axis_size("wide"), lax.axis_size("narrow")
    chips = wide // 2
    core = lax.axis_index("wide") % 2
    slot = lax.axis_index("narrow")
    slots = jnp.reshape(slot, (1,)).astype(jnp.int32)
    same_core = [[i for i in range(wide) if i % 2 == c] for c in range(2)]
    swap = [(i, i ^ 1) for i in range(wide)]
    upward = [(i, i + 1) for i in range(narrow - 1)]
    downward = [(i + 1, i) for i in range(narrow - 1)]
    dw = width // wide
    dh = query_gain.shape[0]
    head = key_weight.shape[1]
    units = gate_weight.shape[1]
    half = width // 2

    def gather_wide(value, axis):
        return lax.all_gather(
            value, "wide", axis=axis, tiled=True, axis_index_groups=same_core
        )

    def sibling(value):
        return lax.ppermute(value, "wide", swap)

    def pair_sum(own, other):
        return (own.astype(F32) + sibling(other).astype(F32)).astype(BF16)

    def scatter_wide(value, axis):
        return lax.psum_scatter(
            value, "wide", scatter_dimension=axis, tiled=True, axis_index_groups=same_core
        )

    def after(value, *others):
        return lax.optimization_barrier((value, *others))[0]

    def gather_rows(value):
        return lax.all_gather(value, "narrow", axis=0, tiled=True)

    def gather_ring(value):
        return pass_on([value] * narrow)

    def pass_on(parts):
        got = [parts[0]]
        for s in range(1, narrow):
            shift = [(i, (i + s) % narrow) for i in range(narrow)]
            got.append(lax.ppermute(parts[s], "narrow", shift))
        return got

    def exchange_z(value):
        parts = value.reshape(narrow, -1, value.shape[-1])
        return lax.all_to_all(parts, "narrow", split_axis=0, concat_axis=0, tiled=True)

    def enter(value):
        value = value.reshape(value.shape[0], value.shape[2], width)
        value = lax.all_to_all(value, "wide", split_axis=0, concat_axis=0, tiled=True)
        return value.reshape(-1, width)

    def leave(value):
        value = value.reshape(wide, -1, width)
        value = lax.all_to_all(value, "wide", split_axis=0, concat_axis=0, tiled=True)
        return value.reshape(wide, 1, -1, width)

    bf, ff = BF16, F32
    pack = call(packing, [((dw, 4 * head + 128), bf)], count=10, flops=10**6, moved=10**6)(
        query_weight, key_weight, value_weight, outproj_weight,
        attn_gain, attnout_gain, ffn_gain, ffnout_gain, query_gain, key_gain,
    )[0]
    wa_mine = gather_wide(pack, 0)
    lengths = seq_lengths[0]
    info = jnp.stack([slot, core, lengths[0], lengths[0] + lengths[1], 0]).astype(jnp.int32)
    queries = gather_ring(query_weight)
    rows = narrow * tokens.shape[2] * wide
    cosine, sine = call(
        rope_tables, [((rows, head // 2), F32)] * 2, smem=(0,), count=1, flops=10**6, moved=2 * 10**6
    )(info)
    own_x = after(enter(tokens), info, cosine, sine, *queries)
    quarter = own_x.shape[0]
    part = quarter // CHUNKS
    every = range(CHUNKS)
    sem = pltpu.SemaphoreType.DMA
    f_scratch = pltpu.VMEM((3, width, units), bf)
    x_all = gather_ring(own_x)
    wf_mine = gather_wide(after(jnp.stack([gate_weight, up_weight, down_weight]), own_x), 1)
    weights = [sibling(after(wa_mine, *x_all)), wa_mine]
    wh_mine = gather_wide(after(jnp.stack(queries), wf_mine), 1)
    own_dy = enter(after(cotangent, own_x))
    many = len(x_all) + len(weights)
    kept = [
        ((rows, width), bf), ((rows, width), bf), ((rows, head), ff), ((rows, head), ff),
        ((rows, rows), ff),
    ]
    (
        xp, xn1, qraw, kraw, probs, wkv, wout, q, k, v, attended, gains, hgain,
        order, pick, *z_parts,
    ) = call(
        functools.partial(attention_forward, wide),
        kept
        + [((width, 2 * head), bf), ((width, head), bf)]
        + [((rows, head), bf)] * 4
        + [((8, width), ff), ((8, head), ff), ((1, width), jnp.int32), ((1, head), jnp.int32)]
        + [((quarter, width), bf)] * narrow,
        scratch=[pltpu.VMEM(*k) for k in kept]
        + [
            pltpu.VMEM((rows, width), bf), pltpu.VMEM((rows, width), bf),
            pltpu.VMEM((width, 4 * head + 128), bf), sem((len(weights),)), sem((7,)),
        ],
        anys=tuple(range(len(x_all), many)), smem=(many,), count=many + 3, far=7,
        flops=3 * 10**9, moved=8 * 10**6,
    )(*x_all, *weights, info, cosine, sine)
    z = pass_on(z_parts)
    mixed, h, *xn2_own = call(
        middle_forward,
        [((quarter, width), ff)] * 2 + [((part, width), bf)] * CHUNKS,
        smem=(narrow + 2,), count=narrow + 3, flops=10**7, moved=2 * 10**6,
    )(*z, xp, gains, slots)
    xn2 = [gather_ring(xn2_own[c]) for c in every]
    wf_other = sibling(after(wf_mine, xn2[0][1], xn2[0][-1]))
    def ffn_ahead(c):
        return call(
            ffn_forward,
            [((narrow * part, width), bf)] + [((narrow * part, units), bf)] * 3
            + [((part, width), bf)] * narrow,
            scratch=[pltpu.VMEM((rows, width), bf)] + [pltpu.VMEM((rows, units), bf)] * 3
            + [
                pltpu.VMEM((rows, width), bf), f_scratch, sem((len(tiles(units, FFN_TILE)), 4)),
                sem((2,)), sem((len(tiles(units, FFN_TILE)) + 1, 3)),
            ],
            anys=(narrow, narrow + 1), count=narrow + 2, far=4, flops=3 * 10**9, moved=16 * 10**6,
        )(*xn2[c], wf_mine, wf_other)

    ahead = []
    for c in every:
        if c:
            xn2[c][0] = after(xn2[c][0], ahead[-1][1])
        ahead.append(ffn_ahead(c))
    xn2_all, act, fa, fb, *m_part = zip(*ahead)
    m = [pass_on([p[c] for p in m_part]) for c in every]
    out_own, d_out, dm_own, turn_term = zip(*[
        call(
            functools.partial(middle_turn, c),
            [((part, width), bf), ((part, width), ff), ((part, width), bf), ((1, width), ff)],
            smem=(narrow + 3,), count=narrow + 5, flops=10**8, moved=4 * 10**6,
        )(*m[c], h, own_dy, order, info, gains)
        for c in every
    ])
    dm = [gather_ring(dm_own[c]) for c in every]

    dm[0][0] = after(dm[0][0], wh_mine)

    def ffn_back(c):
        return call(
            ffn_backward,
            [((narrow * part, width), bf)] + [((narrow * part, units), bf)] * 2
            + [((narrow * part, width), bf)],
            scratch=[f_scratch, sem((6,))],
            anys=(narrow + 2, narrow + 3), smem=(narrow + 4,), count=narrow + 5,
            flops=3 * 10**9, moved=16 * 10**6,
        )(*dm[c], fa[c], fb[c], wf_mine, wf_other, slots)

    back = []
    for c in every:
        if c:
            dm[c][0] = after(dm[c][0], back[-1][1])
        back.append(ffn_back(c))
    dm_all, d_gate, d_up, dxn2_part = zip(*back)
    dxn2 = lax.psum_scatter(
        dxn2_part[0].reshape(narrow, quarter, width), "narrow", scatter_dimension=0, tiled=True
    )
    saved = (*dm_all, *xn2_all, *act, *d_gate, *d_up)

    def ffn_grads(first, *received):
        outs = [((3, half, units), bf)] if received else [((half, units), bf)] * 3
        return call(
            functools.partial(ffn_weight_grads, first),
            outs,
            scratch=[pltpu.VMEM((half, rows), bf)],
            count=5 * CHUNKS + len(received), flops=10**6, moved=10**6,
        )(*saved, *received)

    ffn_other = [sibling(g) for g in ffn_grads(half)]
    ffn_sum = ffn_grads(0, *ffn_other)[0]
    dxn2 = after(dxn2, ffn_sum)
    s_ffn = scatter_wide(ffn_sum, 1)
    left_out = leave(out_own[0])
    d_resid, dz_own, ffn_term, attnout_term = call(
        middle_backward,
        [((quarter, width), ff), ((quarter, width), bf), ((1, width), ff), ((1, width), ff)],
        count=5, flops=10**7, moved=3 * 10**6,
    )(dxn2, d_out[0], h, mixed, gains)
    dz = gather_ring(dz_own)
    wh_other = sibling(after(wh_mine, dz_own))
    dz_all, joined_part, query_term, *joined = call(
        attention_backward,
        [((rows, width), bf), ((rows, 3 * head), bf), ((1, head), ff)]
        + [((quarter, 3 * head), bf)] * narrow,
        scratch=[pltpu.VMEM((rows, head), bf), pltpu.VMEM((rows, rows), bf)],
        smem=(narrow,), count=narrow + 10, flops=2 * 10**9, moved=6 * 10**6,
    )(*dz, slots, wout, qraw, q, k, v, probs, hgain, cosine, sine)
    joined = pass_on(joined)

    def outer(left, right, columns):
        return call(
            weight_grad,
            [((half, columns), bf)] * 2,
            scratch=[pltpu.VMEM((width, left.shape[0]), bf)],
            count=2, flops=2 * width * left.shape[0] * columns, moved=3 * 10**6,
        )(left, right)

    g_query = outer(xn1, joined_part, head)
    g_outproj = outer(dz_all, attended, head)
    joined[0] = after(joined[0], left_out, *g_query, *g_outproj)
    heads = wh_mine.shape[0]
    dx_own, own, other = call(
        last_rows,
        [((quarter, width), bf)] + [((half, 4 * head + 128), bf)] * 2,
        scratch=[
            pltpu.VMEM((heads, width, head), bf), sem((2,)),
            pltpu.VMEM((quarter, width), bf), pltpu.VMEM((quarter, width), bf),
            pltpu.VMEM((quarter, head), ff), pltpu.VMEM((quarter, head // 2), ff),
            pltpu.VMEM((quarter, head // 2), ff), sem((5,)),
        ],
        smem=(14,), anys=(4, 5, 7, 8, 9, 24, 25), count=26, flops=10**9, moved=8 * 10**6,
    )(
        *joined, xp, xn1, d_resid, kraw, cosine, sine, hgain, gains, order, pick, slots,
        attnout_term, ffn_term, *turn_term, query_term, *g_query, *g_outproj, wkv,
        wh_mine, wh_other,
    )

    def scatter_chips(value):
        parts = value.reshape(chips, dw, value.shape[1])
        parts = lax.all_to_all(
            parts, "wide", split_axis=0, concat_axis=0, tiled=True, axis_index_groups=same_core
        )
        return parts.astype(F32).sum(axis=0)

    last = scatter_chips(pair_sum(own, other))
    s_query, s_outproj = last[:, :head], last[:, head : 2 * head]
    last = last[:, 2 * head :].astype(BF16)
    last, s_ffn, dx_own = lax.optimization_barrier((last, s_ffn, dx_own))
    s_ffn = s_ffn.astype(F32)
    left_dx, shared = leave(dx_own), gather_ring(last)
    left_dx, *shared = lax.optimization_barrier((left_dx, *shared))
    small = call(
        finish,
        [((dw, head), ff)] * 2 + [((dw,), ff)] * 4 + [((dh,), ff)] * 2,
        count=narrow, flops=10**6, moved=2 * 10**6,
    )(*shared)
    return (left_out, left_dx, s_query, *small[:2], s_outproj, s_ffn[0], s_ffn[1], s_ffn[2], *small[2:])


def solution(mesh):
    return jax.shard_map(
        on_device,
        mesh=mesh,
        in_specs=(
            P(None, "narrow", "wide", None),
            P(None, "narrow", "wide", None),
            P("wide", None),
            P("wide", "narrow"),
            P("wide", None),
            P("wide", None),
            P("wide", "narrow"),
            P("wide", "narrow"),
            P("wide", "narrow"),
            P("wide", "narrow"),
            P("wide"),
            P("wide"),
            P("wide"),
            P("wide"),
            P("wide"),
            P("wide"),
        ),
        out_specs=(
            P(None, "narrow", "wide", None),
            P(None, "narrow", "wide", None),
            P("wide", "narrow"),
            P("wide", None),
            P("wide", None),
            P("wide", "narrow"),
            P("wide", "narrow"),
            P("wide", "narrow"),
            P("wide", "narrow"),
            P("wide"),
            P("wide"),
            P("wide"),
            P("wide"),
            P("wide"),
            P("wide"),
        ),
        check_vma=False,
    )
```

```python
import functools
import math

import jax
import jax.numpy as jnp
from jax import lax
from jax.experimental import pallas as pl
from jax.experimental.pallas import tpu as pltpu
from jax.sharding import PartitionSpec as P

EPS = 1e-06
SCALE = 0.0625
LOGBASE = math.log(1000000.0)
GELU_C = 0.7978845608028654
GELU_A = 0.044715
F32, BF16 = jnp.float32, jnp.bfloat16
VMEM_LIMIT = 60 * 1024 * 1024
CHUNKS = 1
RING = 4
FFN_TILE = 512


def call(kernel, outs, scratch=(), anys=(), smem=(), count=0, flops=0, moved=0, far=0):
    limit = (16 if moved <= 4 * 10**6 and moved != 10**6 else 60) * 1024 * 1024
    def place(index):
        if index in anys:
            return pl.BlockSpec(memory_space=pl.ANY)
        if index in smem:
            return pl.BlockSpec(memory_space=pltpu.SMEM)
        return pl.BlockSpec(memory_space=pltpu.VMEM)

    return pl.pallas_call(
        kernel,
        out_shape=[jax.ShapeDtypeStruct(s, d) for s, d in outs],
        in_specs=[place(i) for i in range(count)],
        out_specs=[
            pl.BlockSpec(memory_space=pl.ANY if i < far else pltpu.VMEM) for i in range(len(outs))
        ],
        scratch_shapes=list(scratch),
        compiler_params=pltpu.CompilerParams(vmem_limit_bytes=limit),
        cost_estimate=pl.CostEstimate(flops=1, bytes_accessed=1, transcendentals=0),
    )


def mm(a, b):
    return lax.dot_general(a, b, (((1,), (0,)), ((), ())), preferred_element_type=F32)


def mm_nt(a, b):
    return lax.dot_general(a, b, (((1,), (1,)), ((), ())), preferred_element_type=F32)


def mm_tn(a, b):
    return lax.dot_general(a, b, (((0,), (0,)), ((), ())), preferred_element_type=F32)


def root(v):
    return lax.rsqrt(jnp.mean(v * v, axis=-1, keepdims=True) + EPS)


def norm(v, gain):
    return v * root(v) * (1.0 + gain)


def norm_back(v, grad, gain):
    r = root(v)
    e = grad * (1.0 + gain)
    return r * e - v * (r * r * r * jnp.mean(e * v, axis=-1, keepdims=True))


def norm_term(v, grad):
    return jnp.sum(grad * v * root(v), axis=0, keepdims=True)


def rotate(v, cosine, sine):
    half = v.shape[-1] // 2
    a, b = v[:, :half], v[:, half:]
    return jnp.concatenate([a * cosine - b * sine, b * cosine + a * sine], axis=-1)


def rotate_back(v, cosine, sine):
    half = v.shape[-1] // 2
    a, b = v[:, :half], v[:, half:]
    return jnp.concatenate([a * cosine + b * sine, b * cosine - a * sine], axis=-1)


def tiles(extent, size):
    return [(i, min(size, extent - i)) for i in range(0, extent, size)]


def packing(q_ref, k_ref, v_ref, o_ref, g0_ref, g1_ref, g2_ref, g3_ref, g4_ref, g5_ref, out_ref):
    rows, head = q_ref.shape
    for i, ref in enumerate((q_ref, k_ref, v_ref, o_ref)):
        out_ref[:, i * head : (i + 1) * head] = ref[...]
    lane = lax.broadcasted_iota(jnp.int32, (rows, 128), 1)
    columns = jnp.zeros((rows, 128), F32)
    for i, ref in enumerate((g0_ref, g1_ref, g2_ref, g3_ref, g4_ref, g5_ref)):
        n = ref.shape[0]
        same = lax.broadcasted_iota(jnp.int32, (rows, n), 0) == lax.broadcasted_iota(
            jnp.int32, (rows, n), 1
        )
        column = jnp.sum(jnp.where(same, ref[...].astype(F32)[None, :], 0.0), axis=1, keepdims=True)
        columns = jnp.where(lane == i, column, columns)
    out_ref[:, 4 * head :] = columns.astype(BF16)


def one_hot(order, rows):
    index = lax.broadcasted_iota(jnp.int32, (rows, order.shape[1]), 0)
    return jnp.where(index == order, 1.0, 0.0).astype(BF16)


def steps(value, size, count):
    return sum(jnp.where(value >= size * i, 1, 0) for i in range(1, count))


def orders(core, width, head, wide):
    half, dw, dh = width // 2, width // wide, head // wide
    place = lax.broadcasted_iota(jnp.int32, (1, width), 1)
    side = jnp.where(place >= half, 1, 0)
    inner = place - half * side
    chip = steps(inner, dw, wide // 2)
    order = (2 * chip + ((core + side) & 1)) * dw + (inner - chip * dw)
    entry = lax.broadcasted_iota(jnp.int32, (1, head), 1)
    owner = steps(entry, dh, wide)
    chip = steps(owner, 2, wide // 2)
    pick = (((owner & 1) + core) & 1) * half + chip * dw + (entry - owner * dh)
    return order, pick


def segments(position, first, ends):
    segment = jnp.where(position < first, 0, jnp.where(position < ends, 1, 2))
    begin = jnp.where(position < first, 0, jnp.where(position < ends, first, ends))
    return segment, position - begin


def rope_tables(info_ref, cos_ref, sin_ref):
    rows, half = cos_ref.shape
    frequency = jnp.exp(
        lax.broadcasted_iota(jnp.int32, (1, half), 1).astype(F32) * (-1.0 / half) * LOGBASE
    )
    for r, n in tiles(rows, 128):
        position = lax.broadcasted_iota(jnp.int32, (n, 1), 0) + r
        angle = segments(position, info_ref[2], info_ref[3])[1].astype(F32) * frequency
        cos_ref[pl.ds(r, n), :] = jnp.cos(angle)
        sin_ref[pl.ds(r, n), :] = jnp.sin(angle)


def attention_forward(wide, *refs):
    x_refs, weight_refs, refs = refs[:RING], refs[RING:-32], refs[-32:]
    info_ref, cos_ref, sin_ref, *refs = refs
    (
        *far_refs, wkv_ref, wout_ref, q_ref, k_ref, v_ref, att_ref, gains_ref,
        hgain_ref, order_ref, pick_ref,
    ) = refs[:15]
    part_refs, near_refs = refs[15:-10], refs[-10:-5]
    xp_ref, xn1_ref, qraw_ref, kraw_ref, probs_ref = near_refs
    part_ref, x_ref, w_ref, sem, out_sem = refs[-5:]
    leaving = []

    def leave(here, there):
        leaving.append(pltpu.make_async_copy(here, there, out_sem.at[len(leaving)]))
        leaving[-1].start()

    head = q_ref.shape[1]
    rows, width = x_ref.shape
    half = width // 2
    slot, core, first, ends = info_ref[0], info_ref[1], info_ref[2], info_ref[3]
    copies, count = [], len(weight_refs) // 2
    for i, ref in enumerate(weight_refs):
        n = ref.shape[0]
        at = pl.multiple_of(info_ref[4 + i % count] * n + half * (1 - i // count), 16)
        copies.append(pltpu.make_async_copy(ref, w_ref.at[pl.ds(at, n)], sem.at[i]))
        copies[-1].start()
    collect(x_refs, slot, x_ref)
    order, pick = orders(core, width, head, wide)
    order_ref[...] = order
    pick_ref[...] = pick
    choose = one_hot(order, width)
    step = 128
    for r, n in tiles(rows, step):
        xp_ref[pl.ds(r, n), :] = mm(x_ref[pl.ds(r, n), :], choose).astype(BF16)
    leave(xp_ref, far_refs[0])
    for c in copies:
        c.wait()
    columns = w_ref[:, 4 * head :].T
    gains_ref[...] = columns[:8].astype(F32)
    hgain_ref[...] = mm(columns[:8], one_hot(pick, width))
    leave(w_ref.at[:, pl.ds(head, 2 * head)], wkv_ref)
    leave(w_ref.at[:, pl.ds(3 * head, head)], wout_ref)
    for r, n in tiles(rows, step):
        x = xp_ref[pl.ds(r, n), :].astype(F32)
        xn1_ref[pl.ds(r, n), :] = norm(x, gains_ref[0:1, :]).astype(BF16)
    leave(xn1_ref, far_refs[1])
    gq, gk = hgain_ref[4:5, :], hgain_ref[5:6, :]
    raw = mm(xn1_ref[...], w_ref[:, : 3 * head])
    qraw_ref[...] = raw[:, :head]
    kraw_ref[...] = raw[:, head : 2 * head]
    leave(qraw_ref, far_refs[2])
    leave(kraw_ref, far_refs[3])
    v_ref[...] = raw[:, 2 * head :].astype(BF16)
    cosine, sine = cos_ref[...], sin_ref[...]
    q_ref[...] = rotate(norm(raw[:, :head], gq), cosine, sine).astype(BF16)
    k_ref[...] = rotate(norm(raw[:, head : 2 * head], gk), cosine, sine).astype(BF16)
    for r, n in tiles(rows, step):
        s = mm_nt(q_ref[pl.ds(r, n), :], k_ref[...]) * SCALE
        row = lax.broadcasted_iota(jnp.int32, s.shape, 0) + r
        col = lax.broadcasted_iota(jnp.int32, s.shape, 1)
        keep = (segments(row, first, ends)[0] == segments(col, first, ends)[0]) & (col <= row)
        s = jnp.where(keep, s, -1e30)
        e = jnp.exp(s - jnp.max(s, axis=-1, keepdims=True))
        p = e / jnp.sum(e, axis=-1, keepdims=True)
        probs_ref[pl.ds(r, n), :] = p
        att_ref[pl.ds(r, n), :] = mm(p.astype(BF16), v_ref[...]).astype(BF16)
    leave(probs_ref, far_refs[4])
    for r, n in tiles(rows, step):
        part_ref[pl.ds(r, n), :] = mm_nt(
            att_ref[pl.ds(r, n), :], w_ref[:, 3 * head : 4 * head]
        ).astype(BF16)
    hand_out(part_ref, slot, part_refs)
    for c in leaving:
        c.wait()


def hand_out(whole_ref, slot, refs):
    for s, ref in enumerate(refs):
        n = ref.shape[0]
        at = lax.rem(slot + s, len(refs)) * n
        ref[...] = whole_ref[pl.ds(pl.multiple_of(at, n), n), :]


def spread(whole_ref, refs):
    for s, ref in enumerate(refs):
        n = ref.shape[0]
        ref[...] = whole_ref[pl.ds((len(refs) - s) % len(refs) * n, n), :]


def collect(refs, slot, target):
    for s, ref in enumerate(refs):
        n = ref.shape[0]
        at = pl.multiple_of(lax.rem(slot + len(refs) - s, len(refs)) * n, n)
        target[pl.ds(at, n), :] = ref[...]


def total(refs):
    out = refs[0][...].astype(F32)
    for ref in refs[1:]:
        out = out + ref[...].astype(F32)
    return out


def middle_forward(*refs):
    *z_refs, xp_ref, gains_ref, slot_ref, mixed_ref, h_ref = refs[:-CHUNKS]
    n = h_ref.shape[0]
    x = xp_ref[pl.ds(pl.multiple_of(slot_ref[0] * n, n), n), :].astype(F32)
    z = total(z_refs)
    h = x + norm(z, gains_ref[1:2, :])
    mixed_ref[...] = z
    h_ref[...] = h
    xn2 = norm(h, gains_ref[2:3, :]).astype(BF16)
    for c, ref in enumerate(refs[-CHUNKS:]):
        ref[...] = xn2[c * ref.shape[0] : (c + 1) * ref.shape[0]]


def load_weights(sources, target, sem, order):
    half = sources[0].shape[1]
    waits = []
    for i in order:
        pair = [
            pltpu.make_async_copy(
                ref.at[i], target.at[i, pl.ds(j * half, half)], sem.at[2 * i + j]
            )
            for j, ref in enumerate(sources)
        ]
        for c in pair:
            c.start()
        waits.append(lambda pair=pair: [c.wait() for c in pair])
    return waits


def ffn_forward(*refs):
    wm_ref, wo_ref = refs[RING : RING + 2]
    x_out, act_out, fa_out, fb_out, *part_refs = refs[RING + 2 : -9]
    x_ref, act_ref, fa_ref, fb_ref, part_ref, w_ref, sem, down_sem, out_sem = refs[-9:]
    half = wm_ref.shape[1]
    cuts = tiles(act_ref.shape[1], FFN_TILE)
    loads = []
    for t, (f, n) in enumerate(cuts):
        columns = pl.ds(f, n)
        group = [
            pltpu.make_async_copy(
                ref.at[i, :, columns],
                w_ref.at[i, pl.ds(j * half, half), columns],
                sem.at[t, 2 * i + j],
            )
            for i in (0, 1)
            for j, ref in enumerate((wm_ref, wo_ref))
        ]
        for c in group:
            c.start()
        loads.append(group)
    down = [
        pltpu.make_async_copy(ref.at[2], w_ref.at[2, pl.ds(j * half, half)], down_sem.at[j])
        for j, ref in enumerate((wm_ref, wo_ref))
    ]
    for c in down:
        c.start()
    for s in range(RING):
        n = refs[s].shape[0]
        x_ref[s * n : (s + 1) * n] = refs[s][...]
    leaving = [pltpu.make_async_copy(x_ref, x_out, out_sem.at[0, 0])]
    leaving[0].start()
    x = x_ref[...]
    for t, (f, n) in enumerate(cuts):
        columns = pl.ds(f, n)
        for c in loads[t]:
            c.wait()
        gate = mm(x, w_ref[0, :, columns])
        up = mm(x, w_ref[1, :, columns])
        square = gate * gate
        th = jnp.tanh(GELU_C * (gate + GELU_A * (gate * square)))
        bell = 0.5 * (1.0 + th)
        g = gate * bell
        slope = bell + 0.5 * gate * (1.0 - th * th) * (GELU_C * (1.0 + 3.0 * GELU_A * square))
        act_ref[:, columns] = (g * up).astype(BF16)
        fa_ref[:, columns] = (slope * up).astype(BF16)
        fb_ref[:, columns] = g.astype(BF16)
        pairs = ((act_ref, act_out), (fa_ref, fa_out), (fb_ref, fb_out))
        for i, (here, there) in enumerate(pairs):
            c = pltpu.make_async_copy(
                here.at[:, columns], there.at[:, columns], out_sem.at[1 + t, i]
            )
            c.start()
            leaving.append(c)
    for c in down:
        c.wait()
    for d, n in tiles(part_ref.shape[1], 384):
        part_ref[:, pl.ds(d, n)] = mm_nt(act_ref[...], w_ref[2, pl.ds(d, n), :]).astype(BF16)
    spread(part_ref, part_refs)
    for c in leaving:
        c.wait()


def middle_turn(chunk, *refs):
    *m_refs, h_ref, dy_ref, order_ref, info_ref, gains_ref = refs[:-4]
    out_ref, dout_ref, dm_ref, term_ref = refs[-4:]
    n = dm_ref.shape[0]
    choose = one_hot(order_ref[...], h_ref.shape[1])
    m = total(m_refs)
    gain = gains_ref[3:4, :]
    here = pl.ds(chunk * n, n)
    out = (h_ref[here, :] + norm(m, gain)).astype(BF16)
    out_ref[...] = mm_nt(out, choose).astype(BF16)
    position = lax.broadcasted_iota(jnp.int32, (n, 1), 0) + (info_ref[0] * CHUNKS + chunk) * n
    dy = mm(dy_ref[here, :], choose) * jnp.where(position < info_ref[3], 1.0, 0.0)
    dout_ref[...] = dy
    dm_ref[...] = norm_back(m, dy, gain).astype(BF16)
    term_ref[...] = norm_term(m, dy)


def ffn_backward(*refs):
    fa_ref, fb_ref, wm_ref, wo_ref = refs[RING : RING + 4]
    slot_ref, dm_ref, dg_ref, du_ref, out_ref, part_ref, w_ref, sem = refs[RING + 4 :]
    waits = load_weights((wm_ref, wo_ref), w_ref, sem, (2, 0, 1))
    for s in range(RING):
        n = refs[s].shape[0]
        dm_ref[s * n : (s + 1) * n] = refs[s][...]
    waits[0]()
    dm = dm_ref[...]
    for f, n in tiles(dg_ref.shape[1], 256):
        d = mm(dm, w_ref[2, :, pl.ds(f, n)])
        dg_ref[:, pl.ds(f, n)] = (d * fa_ref[:, pl.ds(f, n)].astype(F32)).astype(BF16)
        du_ref[:, pl.ds(f, n)] = (d * fb_ref[:, pl.ds(f, n)].astype(F32)).astype(BF16)
    waits[1]()
    waits[2]()
    for d, n in tiles(part_ref.shape[1], 384):
        part = mm_nt(dg_ref[...], w_ref[0, pl.ds(d, n), :])
        part_ref[:, pl.ds(d, n)] = (part + mm_nt(du_ref[...], w_ref[1, pl.ds(d, n), :])).astype(BF16)
    n = refs[0].shape[0]
    collect([part_ref.at[pl.ds(s * n, n)] for s in range(RING)], slot_ref[0], out_ref)


def weight_grad(left_ref, right_ref, own_ref, other_ref, turned_ref):
    turned_ref[...] = left_ref[...].T
    half, n_right = own_ref.shape
    for r, n in tiles(half, 192):
        for at, out in ((r, own_ref), (half + r, other_ref)):
            grad = mm(turned_ref[pl.ds(at, n), :], right_ref[:, :n_right])
            out[pl.ds(r, n), :] = grad.astype(BF16)


def ffn_weight_grads(first, *refs):
    groups = [refs[CHUNKS * i : CHUNKS * (i + 1)] for i in range(5)]
    dm, xn2, act, dg, du = groups
    *rest, turned_ref = refs[CHUNKS * 5 :]
    half, part = turned_ref.shape[0], dm[0].shape[0]
    received = rest[:3] if len(rest) == 4 else []
    outs = [rest[3].at[i] for i in range(3)] if received else rest
    for i, (left, right) in enumerate(((xn2, dg), (xn2, du), (dm, act))):
        if i != 1:
            for c, ref in enumerate(left):
                turned = ref[:, first : first + half].T
                turned_ref[:, c * part : (c + 1) * part] = turned
        for r, n in tiles(half, 192):
            grad = sum(
                mm(turned_ref[pl.ds(r, n), c * part : (c + 1) * part], right[c][...])
                for c in range(CHUNKS)
            )
            if received:
                grad = grad + received[i][pl.ds(r, n), :].astype(F32)
            outs[i][pl.ds(r, n), :] = grad.astype(BF16)


def load_heads(sources, target, sem):
    half = sources[0].shape[1]
    copies = [
        pltpu.make_async_copy(
            ref, target.at[:, pl.ds(j * half, half), :], sem.at[j]
        )
        for j, ref in enumerate(sources)
    ]
    for c in copies:
        c.start()
    return lambda: [c.wait() for c in copies]


def middle_backward(g_ref, dout_ref, h_ref, mixed_ref, gains_ref, dh_ref, dz_ref, fterm_ref, aterm_ref):
    dxn2 = g_ref[0].astype(F32)
    h, mixed = h_ref[...], mixed_ref[...]
    dh = dout_ref[...] + norm_back(h, dxn2, gains_ref[2:3, :])
    dh_ref[...] = dh
    dz_ref[...] = norm_back(mixed, dh, gains_ref[1:2, :]).astype(BF16)
    fterm_ref[...] = norm_term(h, dxn2)
    aterm_ref[...] = norm_term(mixed, dh)


def attention_backward(*refs):
    (
        slot_ref, wout_ref, qraw_ref, q_ref, k_ref, v_ref, probs_ref, hgain_ref, cos_ref, sin_ref,
        dz_out, dq_ref, term_ref, *out_refs, part_ref, dz_ref, datt_ref, ds_ref, sem,
    ) = refs[RING:]
    rows, head = q_ref.shape
    collect(refs[:RING], slot_ref[0], dz_ref)
    leaving = pltpu.make_async_copy(dz_ref, dz_out, sem.at[0])
    leaving.start()
    datt_ref[...] = mm(dz_ref[...], wout_ref[...]).astype(BF16)
    term = jnp.zeros((1, head), F32)
    for r, n in tiles(rows, 128):
        p = probs_ref[pl.ds(r, n), :]
        dp = mm_nt(datt_ref[pl.ds(r, n), :], v_ref[...])
        ds = (p * (dp - jnp.sum(dp * p, axis=-1, keepdims=True))).astype(BF16)
        ds_ref[pl.ds(r, n), :] = ds
        dq = (mm(ds, k_ref[...]) * SCALE).astype(BF16).astype(F32)
        cosine, sine = cos_ref[pl.ds(r, n), :], sin_ref[pl.ds(r, n), :]
        e = rotate_back(dq, cosine, sine)
        raw = qraw_ref[pl.ds(r, n), :]
        term = term + norm_term(raw, e)
        part_ref[pl.ds(r, n), :head] = norm_back(raw, e, hgain_ref[4:5, :]).astype(BF16)
    term_ref[...] = term
    part_ref[:, head : 2 * head] = (mm_tn(ds_ref[...], q_ref[...]) * SCALE).astype(BF16)
    part_ref[:, 2 * head :] = mm_tn(probs_ref[...].astype(BF16), datt_ref[...]).astype(BF16)
    hand_out(part_ref, slot_ref[0], out_refs)
    dq_ref[...] = part_ref[:, :head]
    leaving.wait()


def last_rows(
    g0_ref, g1_ref, g2_ref, g3_ref, xp_ref, xn1_ref, dh_ref, kraw_ref, cos_ref, sin_ref, hgain_ref, gains_ref, order_ref,
    pick_ref, slot_ref, t1_ref, t2_ref, t3_ref, qterm_ref, qm_ref, qo_ref, om_ref, oo_ref, w_ref, hm_ref, ho_ref,
    out_ref, own_ref, other_ref,
    wq_ref, hsem, x_here, xn1_here, raw_here, cos_here, sin_here, row_sem,
):
    head = kraw_ref.shape[1]
    n, width = dh_ref.shape
    half = width // 2
    arrived = load_heads((hm_ref, ho_ref), wq_ref, hsem)
    here = pl.ds(pl.multiple_of(slot_ref[0] * n, n), n)
    rows = [
        pltpu.make_async_copy(ref.at[here], target, row_sem.at[i])
        for i, (ref, target) in enumerate((
            (kraw_ref, raw_here), (cos_ref, cos_here), (sin_ref, sin_here), (xn1_ref, xn1_here),
            (xp_ref, x_here),
        ))
    ]
    for c in rows:
        c.start()
    g_refs = (g0_ref, g1_ref, g2_ref, g3_ref)
    joined = sum(ref[:, head:].astype(F32) for ref in g_refs)
    dk = joined[:, :head].astype(BF16).astype(F32)
    for c in rows:
        c.wait()
    e = rotate_back(dk, cos_here[...], sin_here[...])
    raw = raw_here[...]
    kterm = norm_term(raw, e)
    dkr = norm_back(raw, e, hgain_ref[5:6, :]).astype(BF16)
    dkv = jnp.concatenate([dkr, joined[:, head:].astype(BF16)], axis=1)
    dxn1 = mm_nt(dkv, w_ref[...])
    arrived()
    for i, ref in enumerate(g_refs):
        dxn1 = dxn1 + mm_nt(ref[:, :head], wq_ref[i])
    x = x_here[...].astype(F32)
    dx = (dh_ref[...] + norm_back(x, dxn1, gains_ref[0:1, :])).astype(BF16)
    term = norm_term(x, dxn1)
    choose = one_hot(order_ref[...], width)
    out_ref[...] = mm_nt(dx, choose).astype(BF16)
    grad = mm_tn(xn1_here[...], dkv)
    for i, (mine, others) in enumerate(((qm_ref, qo_ref), (om_ref, oo_ref))):
        own_ref[:, i * head : (i + 1) * head] = mine[...]
        other_ref[:, i * head : (i + 1) * head] = others[...]
    own_ref[:, 2 * head : 4 * head] = grad[:half].astype(BF16)
    other_ref[:, 2 * head : 4 * head] = grad[half:].astype(BF16)
    small = jnp.concatenate([qterm_ref[...], kterm, jnp.zeros((6, head), F32)], axis=0)
    small = mm_nt(small.astype(BF16), one_hot(pick_ref[...], width))
    terms = [term, t1_ref[...], t2_ref[...], t3_ref[...], small[0:2], jnp.zeros((122, width), F32)]
    terms = jnp.concatenate(terms, axis=0).T
    own_ref[:, 4 * head :] = terms[:half].astype(BF16)
    other_ref[:, 4 * head :] = terms[half:].astype(BF16)


def finish(*refs):
    key_ref, value_ref, *rows = refs[RING:]
    head = key_ref.shape[1]
    value = total(refs[:RING])
    key_ref[...] = value[:, :head]
    value_ref[...] = value[:, head : 2 * head]
    n = value.shape[0]
    same = lax.broadcasted_iota(jnp.int32, (n, n), 0) == lax.broadcasted_iota(jnp.int32, (n, n), 1)
    for i, ref in enumerate(rows):
        column = value[:, 2 * head + i : 2 * head + i + 1]
        row = jnp.sum(jnp.where(same, column, 0.0), axis=0)
        ref[...] = row[: ref.shape[0]]


def on_device(
    tokens,
    cotangent,
    seq_lengths,
    query_weight,
    key_weight,
    value_weight,
    outproj_weight,
    gate_weight,
    up_weight,
    down_weight,
    attn_gain,
    attnout_gain,
    ffn_gain,
    ffnout_gain,
    query_gain,
    key_gain,
):
    width = tokens.shape[3]
    wide, narrow = lax.axis_size("wide"), lax.axis_size("narrow")
    chips = wide // 2
    core = lax.axis_index("wide") % 2
    slot = lax.axis_index("narrow")
    slots = jnp.reshape(slot, (1,)).astype(jnp.int32)
    same_core = [[i for i in range(wide) if i % 2 == c] for c in range(2)]
    swap = [(i, i ^ 1) for i in range(wide)]
    upward = [(i, i + 1) for i in range(narrow - 1)]
    downward = [(i + 1, i) for i in range(narrow - 1)]
    dw = width // wide
    dh = query_gain.shape[0]
    head = key_weight.shape[1]
    units = gate_weight.shape[1]
    half = width // 2

    def gather_wide(value, axis):
        return lax.all_gather(
            value, "wide", axis=axis, tiled=True, axis_index_groups=same_core
        )

    def sibling(value):
        return lax.ppermute(value, "wide", swap)

    def pair_sum(own, other):
        return (own.astype(F32) + sibling(other).astype(F32)).astype(BF16)

    def scatter_wide(value, axis):
        return lax.psum_scatter(
            value, "wide", scatter_dimension=axis, tiled=True, axis_index_groups=same_core
        )

    def after(value, *others):
        return lax.optimization_barrier((value, *others))[0]

    def gather_rows(value):
        return lax.all_gather(value, "narrow", axis=0, tiled=True)

    def gather_ring(value):
        return pass_on([value] * narrow)

    def pass_on(parts):
        got = [parts[0]]
        for s in range(1, narrow):
            shift = [(i, (i + s) % narrow) for i in range(narrow)]
            got.append(lax.ppermute(parts[s], "narrow", shift))
        return got

    def exchange_z(value):
        parts = value.reshape(narrow, -1, value.shape[-1])
        return lax.all_to_all(parts, "narrow", split_axis=0, concat_axis=0, tiled=True)

    def enter(value):
        value = value.reshape(value.shape[0], value.shape[2], width)
        value = lax.all_to_all(value, "wide", split_axis=0, concat_axis=0, tiled=True)
        return value.reshape(-1, width)

    def leave(value):
        value = value.reshape(wide, -1, width)
        value = lax.all_to_all(value, "wide", split_axis=0, concat_axis=0, tiled=True)
        return value.reshape(wide, 1, -1, width)

    bf, ff = BF16, F32
    pack = call(packing, [((dw, 4 * head + 128), bf)], count=10, flops=10**6, moved=10**6)(
        query_weight, key_weight, value_weight, outproj_weight,
        attn_gain, attnout_gain, ffn_gain, ffnout_gain, query_gain, key_gain,
    )[0]
    wa_mine = gather_wide(pack, 0)
    lengths = seq_lengths[0]
    info = jnp.stack([slot, core, lengths[0], lengths[0] + lengths[1], 0]).astype(jnp.int32)
    queries = gather_ring(query_weight)
    rows = narrow * tokens.shape[2] * wide
    cosine, sine = call(
        rope_tables, [((rows, head // 2), F32)] * 2, smem=(0,), count=1, flops=10**6, moved=2 * 10**6
    )(info)
    own_x = after(enter(tokens), info, cosine, sine, *queries)
    quarter = own_x.shape[0]
    part = quarter // CHUNKS
    every = range(CHUNKS)
    sem = pltpu.SemaphoreType.DMA
    f_scratch = pltpu.VMEM((3, width, units), bf)
    x_all = gather_ring(own_x)
    wf_mine = gather_wide(after(jnp.stack([gate_weight, up_weight, down_weight]), own_x), 1)
    weights = [sibling(after(wa_mine, *x_all)), wa_mine]
    wh_mine = gather_wide(after(jnp.stack(queries), wf_mine), 1)
    own_dy = enter(after(cotangent, own_x))
    many = len(x_all) + len(weights)
    kept = [
        ((rows, width), bf), ((rows, width), bf), ((rows, head), ff), ((rows, head), ff),
        ((rows, rows), ff),
    ]
    (
        xp, xn1, qraw, kraw, probs, wkv, wout, q, k, v, attended, gains, hgain,
        order, pick, *z_parts,
    ) = call(
        functools.partial(attention_forward, wide),
        kept
        + [((width, 2 * head), bf), ((width, head), bf)]
        + [((rows, head), bf)] * 4
        + [((8, width), ff), ((8, head), ff), ((1, width), jnp.int32), ((1, head), jnp.int32)]
        + [((quarter, width), bf)] * narrow,
        scratch=[pltpu.VMEM(*k) for k in kept]
        + [
            pltpu.VMEM((rows, width), bf), pltpu.VMEM((rows, width), bf),
            pltpu.VMEM((width, 4 * head + 128), bf), sem((len(weights),)), sem((7,)),
        ],
        anys=tuple(range(len(x_all), many)), smem=(many,), count=many + 3, far=7,
        flops=3 * 10**9, moved=8 * 10**6,
    )(*x_all, *weights, info, cosine, sine)
    z = pass_on(z_parts)
    mixed, h, *xn2_own = call(
        middle_forward,
        [((quarter, width), ff)] * 2 + [((part, width), bf)] * CHUNKS,
        smem=(narrow + 2,), count=narrow + 3, flops=10**7, moved=2 * 10**6,
    )(*z, xp, gains, slots)
    xn2 = [gather_ring(xn2_own[c]) for c in every]
    wf_other = sibling(after(wf_mine, xn2[0][1], xn2[0][-1]))
    def ffn_ahead(c):
        return call(
            ffn_forward,
            [((narrow * part, width), bf)] + [((narrow * part, units), bf)] * 3
            + [((part, width), bf)] * narrow,
            scratch=[pltpu.VMEM((rows, width), bf)] + [pltpu.VMEM((rows, units), bf)] * 3
            + [
                pltpu.VMEM((rows, width), bf), f_scratch, sem((len(tiles(units, FFN_TILE)), 4)),
                sem((2,)), sem((len(tiles(units, FFN_TILE)) + 1, 3)),
            ],
            anys=(narrow, narrow + 1), count=narrow + 2, far=4, flops=3 * 10**9, moved=16 * 10**6,
        )(*xn2[c], wf_mine, wf_other)

    ahead = []
    for c in every:
        if c:
            xn2[c][0] = after(xn2[c][0], ahead[-1][1])
        ahead.append(ffn_ahead(c))
    xn2_all, act, fa, fb, *m_part = zip(*ahead)
    m = [pass_on([p[c] for p in m_part]) for c in every]
    out_own, d_out, dm_own, turn_term = zip(*[
        call(
            functools.partial(middle_turn, c),
            [((part, width), bf), ((part, width), ff), ((part, width), bf), ((1, width), ff)],
            smem=(narrow + 3,), count=narrow + 5, flops=10**8, moved=4 * 10**6,
        )(*m[c], h, own_dy, order, info, gains)
        for c in every
    ])
    dm = [gather_ring(dm_own[c]) for c in every]

    dm[0][0] = after(dm[0][0], wh_mine)

    def ffn_back(c):
        return call(
            ffn_backward,
            [((narrow * part, width), bf)] + [((narrow * part, units), bf)] * 2
            + [((narrow * part, width), bf)],
            scratch=[pltpu.VMEM((rows, width), bf), f_scratch, sem((6,))],
            anys=(narrow + 2, narrow + 3), smem=(narrow + 4,), count=narrow + 5,
            flops=3 * 10**9, moved=16 * 10**6,
        )(*dm[c], fa[c], fb[c], wf_mine, wf_other, slots)

    back = []
    for c in every:
        if c:
            dm[c][0] = after(dm[c][0], back[-1][1])
        back.append(ffn_back(c))
    dm_all, d_gate, d_up, dxn2_part = zip(*back)
    dxn2 = lax.psum_scatter(
        dxn2_part[0].reshape(narrow, quarter, width), "narrow", scatter_dimension=0, tiled=True
    )
    saved = (*dm_all, *xn2_all, *act, *d_gate, *d_up)

    def ffn_grads(first, *received):
        outs = [((3, half, units), bf)] if received else [((half, units), bf)] * 3
        return call(
            functools.partial(ffn_weight_grads, first),
            outs,
            scratch=[pltpu.VMEM((half, rows), bf)],
            count=5 * CHUNKS + len(received), flops=10**6, moved=10**6,
        )(*saved, *received)

    ffn_other = [sibling(g) for g in ffn_grads(half)]
    ffn_sum = ffn_grads(0, *ffn_other)[0]
    dxn2 = after(dxn2, ffn_sum)
    s_ffn = scatter_wide(ffn_sum, 1)
    left_out = leave(out_own[0])
    d_resid, dz_own, ffn_term, attnout_term = call(
        middle_backward,
        [((quarter, width), ff), ((quarter, width), bf), ((1, width), ff), ((1, width), ff)],
        count=5, flops=10**7, moved=3 * 10**6,
    )(dxn2, d_out[0], h, mixed, gains)
    dz = gather_ring(dz_own)
    wh_other = sibling(after(wh_mine, dz_own))
    dz_all, dq_raw, query_term, *joined = call(
        attention_backward,
        [((rows, width), bf), ((rows, head), bf), ((1, head), ff)]
        + [((quarter, 3 * head), bf)] * narrow,
        scratch=[
            pltpu.VMEM((rows, 3 * head), bf), pltpu.VMEM((rows, width), bf),
            pltpu.VMEM((rows, head), bf), pltpu.VMEM((rows, rows), bf), sem((1,)),
        ],
        smem=(narrow,), count=narrow + 10, far=1, flops=2 * 10**9, moved=6 * 10**6,
    )(*dz, slots, wout, qraw, q, k, v, probs, hgain, cosine, sine)
    joined = pass_on(joined)

    def outer(left, right, columns):
        return call(
            weight_grad,
            [((half, columns), bf)] * 2,
            scratch=[pltpu.VMEM((width, left.shape[0]), bf)],
            count=2, flops=2 * width * left.shape[0] * columns, moved=3 * 10**6,
        )(left, right)

    g_query = outer(xn1, dq_raw, head)
    g_outproj = outer(dz_all, attended, head)
    joined[0] = after(joined[0], left_out, *g_query, *g_outproj)
    heads = wh_mine.shape[0]
    dx_own, own, other = call(
        last_rows,
        [((quarter, width), bf)] + [((half, 4 * head + 128), bf)] * 2,
        scratch=[
            pltpu.VMEM((heads, width, head), bf), sem((2,)),
            pltpu.VMEM((quarter, width), bf), pltpu.VMEM((quarter, width), bf),
            pltpu.VMEM((quarter, head), ff), pltpu.VMEM((quarter, head // 2), ff),
            pltpu.VMEM((quarter, head // 2), ff), sem((5,)),
        ],
        smem=(14,), anys=(4, 5, 7, 8, 9, 24, 25), count=26, flops=10**9, moved=8 * 10**6,
    )(
        *joined, xp, xn1, d_resid, kraw, cosine, sine, hgain, gains, order, pick, slots,
        attnout_term, ffn_term, *turn_term, query_term, *g_query, *g_outproj, wkv,
        wh_mine, wh_other,
    )

    def scatter_chips(value):
        parts = value.reshape(chips, dw, value.shape[1])
        parts = lax.all_to_all(
            parts, "wide", split_axis=0, concat_axis=0, tiled=True, axis_index_groups=same_core
        )
        return parts.astype(F32).sum(axis=0)

    last = scatter_chips(pair_sum(own, other))
    s_query, s_outproj = last[:, :head], last[:, head : 2 * head]
    last = last[:, 2 * head :].astype(BF16)
    last, s_ffn, dx_own = lax.optimization_barrier((last, s_ffn, dx_own))
    s_ffn = s_ffn.astype(F32)
    left_dx, shared = leave(dx_own), gather_ring(last)
    left_dx, *shared = lax.optimization_barrier((left_dx, *shared))
    small = call(
        finish,
        [((dw, head), ff)] * 2 + [((dw,), ff)] * 4 + [((dh,), ff)] * 2,
        count=narrow, flops=10**6, moved=2 * 10**6,
    )(*shared)
    return (left_out, left_dx, s_query, *small[:2], s_outproj, s_ffn[0], s_ffn[1], s_ffn[2], *small[2:])


def solution(mesh):
    return jax.shard_map(
        on_device,
        mesh=mesh,
        in_specs=(
            P(None, "narrow", "wide", None),
            P(None, "narrow", "wide", None),
            P("wide", None),
            P("wide", "narrow"),
            P("wide", None),
            P("wide", None),
            P("wide", "narrow"),
            P("wide", "narrow"),
            P("wide", "narrow"),
            P("wide", "narrow"),
            P("wide"),
            P("wide"),
            P("wide"),
            P("wide"),
            P("wide"),
            P("wide"),
        ),
        out_specs=(
            P(None, "narrow", "wide", None),
            P(None, "narrow", "wide", None),
            P("wide", "narrow"),
            P("wide", None),
            P("wide", None),
            P("wide", "narrow"),
            P("wide", "narrow"),
            P("wide", "narrow"),
            P("wide", "narrow"),
            P("wide"),
            P("wide"),
            P("wide"),
            P("wide"),
            P("wide"),
            P("wide"),
        ),
        check_vma=False,
    )
```
